128 devices in a mesh: rep: 32 (over z_hi, x, y), fsdp: 4 (over z_lo, core).
Axes of the slice: x: 4, y: 4, z: 4 (z_hi: 2, z_lo: 2; z = z_hi * 2 + z_lo), core: 2. Of those that a mesh axis runs over, the one named last changes fastest.
Arguments:
- grads: bfloat16 [32, 4, 256, 2, 8192], P('rep', 'fsdp'), may hold values from -6 to 6
- momentum: float32 [32, 256, 2, 8192], P('rep', 'fsdp'), may hold values from -6 to 6
Outputs:
- new_momentum: float32 [32, 256, 2, 8192], P('rep', 'fsdp')
- update: float32 [256, 2, 8192], P('fsdp')
The draws below stay inside these ranges and needn't reach their ends.
All inputs are finite; a program needn't handle non-finite values.
Results may differ from the reference program's by a relative error of at most 0.0003.
Values sent between devices are 32-bit elements; how exact they have to be, the bound alone decides.
No kernel may reach another device: no remote copies, remote signals or barrier semaphores. Data moves between devices by JAX's collectives and lax.ppermute only.
A program may use at most 128 MiB of HBM per device.

```python
import math
import jax
import jax.numpy as jnp
from jax import lax

D = 8192
MATS = 2
SPAN = 64
BAND = 16
ROWS = 256
N_REP = 32
N_FSDP = 4


def raised(drawn, stream_key, source, target, shards_of, factor):
    def block_of(position):
        return (jnp.arange(drawn.shape[position]) // (drawn.shape[position] // shards_of)).reshape((-1,) + (1,) * (drawn.ndim - 1 - position))

    near = jax.random.permutation(stream_key, shards_of)[block_of(target)]
    second = (block_of(target) + shards_of // 2) % shards_of
    return jnp.where((block_of(source) == near) | (block_of(source) == second), factor * drawn, drawn)


def steps_of(rng, extent, split, smallest, high):
    gain = 1.0
    for axis_at, parts in split:
        steps = jax.random.uniform(jax.random.fold_in(jax.random.fold_in(rng, 6), axis_at), (parts,), jnp.float32, smallest / len(split), high / len(split))
        gain = gain * jnp.repeat(jnp.exp(steps), extent[axis_at] // parts).reshape((-1,) + (1,) * (len(extent) - 1 - axis_at))
    return gain


def noise(stream_key, shape, spread, reach, shards=(), held_as=jnp.bfloat16):
    factor_of = steps_of(stream_key, shape, shards, -0.22, 0.18) if shards else 1.0
    entries = jax.random.normal(stream_key, shape, jnp.float32) * spread * factor_of
    return jnp.minimum(jnp.maximum(entries, -reach), reach).astype(held_as)


def gaussian_with(own_key, dims, spread, most, cuts, heavy, held_as=jnp.bfloat16):
    values = spread * jax.random.normal(own_key, dims, jnp.float32)
    if cuts:
        values = values * steps_of(own_key, dims, cuts, -0.22, 0.18)
    return jnp.clip(raised(values, jax.random.fold_in(own_key, 3), *heavy), -most, most).astype(held_as)


def setup_inputs(seed: int = 0) -> dict:
    key_list = jax.random.split(jax.random.key(seed), 3)
    return {
        "grads": gaussian_with(key_list[0], (N_REP, N_FSDP, ROWS, MATS, D), 1.0, 6.0, ((0, 32), (1, 4)), (1, 2, 4, 2.0)),
        "momentum": noise(key_list[1], (N_REP, ROWS, MATS, D), 1.0, 6.0, ((0, 32), (1, 4)), jnp.float32),
    }


momentum_decay = 0.9

def cosine_basis():
    frequency = jnp.arange(BAND, dtype=jnp.int32)
    positions = jnp.arange(SPAN, dtype=jnp.int32)
    angles = (frequency[:, None] * (2 * positions[None, :] + 1)).astype(jnp.float32) * (math.pi / (2 * SPAN))
    factors = jnp.where(frequency == 0, math.sqrt(1.0 / SPAN), math.sqrt(2.0 / SPAN)).astype(jnp.float32)
    return factors[:, None] * jnp.cos(angles)

def forward_band(field, basis):
    block_count = field.shape[0] // SPAN
    mat_count = field.shape[1]
    column_blocks = field.shape[2] // SPAN
    blocked = field.reshape(block_count, SPAN, mat_count, field.shape[2])
    low_rows = jnp.einsum('pn,anmd->apmd', basis, blocked, precision=lax.Precision.HIGHEST)
    pieces = low_rows.reshape(block_count, BAND, mat_count, column_blocks, SPAN)
    return jnp.einsum('apmjc,qc->apmqj', pieces, basis, precision=lax.Precision.HIGHEST)

def inverse_band(band, basis):
    block_count = band.shape[0]
    mat_count = band.shape[2]
    column_blocks = band.shape[4]
    wide = jnp.einsum('apmqj,qc->apmjc', band, basis, precision=lax.Precision.HIGHEST)
    merged = wide.reshape(block_count, BAND, mat_count, column_blocks * SPAN)
    full = jnp.einsum('pn,apmd->anmd', basis, merged, precision=lax.Precision.HIGHEST)
    return full.reshape(block_count * SPAN, mat_count, column_blocks * SPAN)

def reference(grads, momentum):
    basis = cosine_basis()

    def per_replica(inputs):
        grad_parts, moment_old = inputs
        summed = lax.optimization_barrier(jnp.sum(grad_parts.astype(jnp.float32), axis=0))
        moment = momentum_decay * moment_old + summed
        band = forward_band(moment, basis)
        return (moment - inverse_band(band, basis), band)
    new_momentum, bands = lax.map(per_replica, (grads, momentum))
    mean_band = lax.optimization_barrier(jnp.sum(bands, axis=0)) / N_REP
    return (new_momentum, inverse_band(mean_band, basis))
```

```python
import functools
import math

import jax
import jax.numpy as jnp
import ml_dtypes
import numpy as np
from jax import lax
from jax.experimental import pallas as pl
from jax.experimental.pallas import tpu as pltpu
from jax.sharding import PartitionSpec as P

SPAN = 64
BAND = 16
LANES = 128
GROUP = 8
QUANTUM = 2 * GROUP
DECAY = 0.9
HIGH = (SPAN - BAND) * GROUP
LOW = BAND * GROUP
QUARTER = LOW // 4
PAYLOAD = 2 * HIGH + 3 * 2 * QUARTER
VMEM = 40 * 1024 * 1024


def dct(order):
    q = np.arange(order)[:, None]
    n = np.arange(order)[None, :]
    scale = np.where(q == 0, math.sqrt(1.0 / order), math.sqrt(2.0 / order))
    return scale * np.cos(math.pi * (2 * n + 1) * q / (2 * order))


def split_constant(a):
    high = a.astype(ml_dtypes.bfloat16)
    return high, (a - high.astype(np.float64)).astype(ml_dtypes.bfloat16)


def constants():
    t = dct(SPAN)
    rows = np.kron(t, np.eye(GROUP))
    lanes = np.kron(np.eye(8), t.T)
    coef = np.arange(512) % SPAN
    order = np.concatenate([np.flatnonzero(coef >= BAND), np.flatnonzero(coef < BAND)])
    mats = split_constant(rows) + split_constant(lanes[:, order])
    return [jnp.asarray(a) for a in mats]


def split(x):
    high = x.astype(jnp.bfloat16)
    return high, (x - high.astype(jnp.float32)).astype(jnp.bfloat16)


def dot3(a, b, dims):
    def one(u, v):
        return lax.dot_general(u, v, ((dims[:1], dims[1:]), ((), ())), preferred_element_type=jnp.float32)
    return one(a[0], b[0]) + (one(a[0], b[1]) + one(a[1], b[0]))


def to_wide(x):
    parts = [x[:, g * GROUP : (g + 1) * GROUP, :].reshape(SPAN * GROUP, LANES) for g in range(2)]
    return jnp.concatenate(parts, axis=1)


def store_wide(ref, x, base=None):
    for g in range(2):
        part = x[:, g * LANES : (g + 1) * LANES].reshape(SPAN, GROUP, LANES)
        at = (slice(None), slice(g * GROUP, (g + 1) * GROUP), slice(None))
        ref[at] = part if base is None else base[at] + part


def quarters(x):
    groups = []
    for g in range(2):
        lane = slice(g * LANES, (g + 1) * LANES)
        groups.append(jnp.concatenate([x[i * QUARTER : (i + 1) * QUARTER, lane] for i in range(4)], axis=1))
    return jnp.concatenate(groups, axis=0)


def unquarters(x):
    groups = []
    for g in range(2):
        row = slice(g * QUARTER, (g + 1) * QUARTER)
        groups.append(jnp.concatenate([x[row, i * LANES : (i + 1) * LANES] for i in range(4)], axis=0))
    return jnp.concatenate(groups, axis=1)


def cast_kernel(place, g_ref, out_ref):
    out_ref[...] = g_ref[...].astype(jnp.float32)


def encode(g_ref, r_ref, th, tl, wh, wl, pay_ref, band_ref):
    x = to_wide(g_ref[...].astype(jnp.float32) + r_ref[...])
    c = dot3((th[...], tl[...]), split(x), (1, 0))
    w = dot3(split(quarters(c[:LOW])), (wh[...], wl[...]), (1, 0))
    pay_ref[0:HIGH, :] = c[LOW:, :LANES]
    pay_ref[HIGH : 2 * HIGH, :] = c[LOW:, LANES:]
    for i in range(3):
        at = 2 * HIGH + i * 2 * QUARTER
        pay_ref[at : at + 2 * QUARTER, :] = w[:, i * LANES : (i + 1) * LANES]
    band_ref[...] = w[:, 3 * LANES :].reshape(band_ref.shape)


def encode_kernel(n, place, g_ref, r_ref, th, tl, wh, wl, *outs):
    step = pl.program_id(0)
    for k in range(n):
        @pl.when(step == k)
        def _(k=k):
            encode(g_ref, r_ref, th, tl, wh, wl, outs[k], outs[n])


def project(band, th, tl, wh, wl):
    low = dot3(split(band), (wh[:, 3 * LANES :], wl[:, 3 * LANES :]), (1, 1))
    return dot3((th[:LOW], tl[:LOW]), split(unquarters(low)), (0, 0))


def base_kernel(place, m_ref, g_ref, r_ref, th, tl, wh, wl, out_ref, band_ref):
    x = to_wide(DECAY * m_ref[...] + (g_ref[...].astype(jnp.float32) + r_ref[...]))
    c = dot3((th[:LOW], tl[:LOW]), split(x), (1, 0))
    band = dot3(split(quarters(c)), (wh[:, 3 * LANES :], wl[:, 3 * LANES :]), (1, 0))
    band_ref[...] = band.reshape(band_ref.shape)
    store_wide(out_ref, x - project(band, th, tl, wh, wl))


def decode_kernel(pay_ref, th, tl, wh, wl, base_ref, out_ref):
    at = 2 * HIGH
    w = jnp.concatenate([pay_ref[at + i * 2 * QUARTER : at + (i + 1) * 2 * QUARTER, :] for i in range(3)], axis=1)
    low = dot3(split(w), (wh[:, : 3 * LANES], wl[:, : 3 * LANES]), (1, 1))
    high = jnp.concatenate([pay_ref[:HIGH, :], pay_ref[HIGH : 2 * HIGH, :]], axis=1)
    x = jnp.concatenate([unquarters(low), high], axis=0)
    store_wide(out_ref, dot3((th[...], tl[...]), split(x), (0, 0)), base_ref)


def update_kernel(scale, band_ref, th, tl, wh, wl, out_ref):
    band = band_ref[...].reshape(2 * QUARTER, LANES) * scale
    store_wide(out_ref, project(band, th, tl, wh, wl))


def params():
    return pltpu.CompilerParams(vmem_limit_bytes=VMEM)


def whole(shape):
    return pl.BlockSpec(shape, lambda *_: (0,) * len(shape))


MATRICES = [whole((512, 512))] * 4


def cast(place, g, first, count, slot):
    return pl.pallas_call(
        cast_kernel,
        grid_spec=pltpu.PrefetchScalarGridSpec(
            num_scalar_prefetch=1,
            grid=(count,),
            in_specs=[pl.BlockSpec((SPAN, QUANTUM, LANES), lambda i, p: (p[slot], first + i, 0))],
            out_specs=pl.BlockSpec((SPAN, QUANTUM, LANES), lambda i, p: (0, i, 0)),
        ),
        out_shape=jax.ShapeDtypeStruct((SPAN, count * QUANTUM, LANES), jnp.float32),
        compiler_params=params(),
    )(place, g)


def encoded(place, g, received, first, count, slot, mats):
    out = pl.pallas_call(
        functools.partial(encode_kernel, count),
        grid_spec=pltpu.PrefetchScalarGridSpec(
            num_scalar_prefetch=1,
            grid=(count,),
            in_specs=[
                pl.BlockSpec((SPAN, QUANTUM, LANES), lambda i, p: (p[slot], first + i, 0)),
                pl.BlockSpec((SPAN, QUANTUM, LANES), lambda i, p: (0, i, 0)),
            ]
            + MATRICES,
            out_specs=[whole((PAYLOAD, LANES))] * count
            + [pl.BlockSpec((2, QUARTER, LANES), lambda i, p: (i, 0, 0))],
        ),
        out_shape=[jax.ShapeDtypeStruct((PAYLOAD, LANES), jnp.float32)] * count
        + [jax.ShapeDtypeStruct((2 * count, QUARTER, LANES), jnp.float32)],
        compiler_params=params(),
    )(place, g, received, *mats)
    return out[:count], out[count]


def based(place, m, g, received, slot, mats):
    count = m.shape[1] // QUANTUM
    block = (SPAN, QUANTUM, LANES)
    return pl.pallas_call(
        base_kernel,
        grid_spec=pltpu.PrefetchScalarGridSpec(
            num_scalar_prefetch=1,
            grid=(count,),
            in_specs=[
                pl.BlockSpec(block, lambda i, p: (0, i, 0)),
                pl.BlockSpec(block, lambda i, p: (p[slot], i, 0)),
                pl.BlockSpec(block, lambda i, p: (0, i, 0)),
            ]
            + MATRICES,
            out_specs=[
                pl.BlockSpec(block, lambda i, p: (0, i, 0)),
                pl.BlockSpec((2, QUARTER, LANES), lambda i, p: (i, 0, 0)),
            ],
        ),
        out_shape=[
            jax.ShapeDtypeStruct(m.shape, jnp.float32),
            jax.ShapeDtypeStruct((2 * count, QUARTER, LANES), jnp.float32),
        ],
        compiler_params=params(),
    )(place, m, g, received, *mats)


def decoded(payload, base, at, mats):
    block = pl.BlockSpec((SPAN, QUANTUM, LANES), lambda i: (0, at, 0))
    return pl.pallas_call(
        decode_kernel,
        grid=(1,),
        in_specs=[whole((PAYLOAD, LANES))] + MATRICES + [block],
        out_specs=block,
        out_shape=jax.ShapeDtypeStruct(base.shape, jnp.float32),
        input_output_aliases={5: 0},
        compiler_params=params(),
    )(payload, *mats, base)


def updated(band, scale, shape, mats):
    count = shape[1] // QUANTUM
    return pl.pallas_call(
        functools.partial(update_kernel, scale),
        grid=(count,),
        in_specs=[pl.BlockSpec((2, QUARTER, LANES), lambda i: (i, 0, 0))] + MATRICES,
        out_specs=pl.BlockSpec((SPAN, QUANTUM, LANES), lambda i: (0, i, 0)),
        out_shape=jax.ShapeDtypeStruct(shape, jnp.float32),
        compiler_params=params(),
    )(band, *mats)


def tiles(x):
    rows, mats, width = x.shape
    x = x.reshape(rows, mats, width // LANES, LANES).transpose(0, 2, 1, 3)
    return x.reshape(rows, mats * width // LANES, LANES)


def untiles(x, mats):
    rows, places, _ = x.shape
    x = x.reshape(rows, places // mats, mats, LANES).transpose(0, 2, 1, 3)
    return x.reshape(rows, mats, places // mats * LANES)


def tie(*arrays):
    return lax.optimization_barrier(arrays)


def per_device(grads, momentum):
    rep_count = lax.axis_size("rep")
    mat_count = grads.shape[3]
    mats = constants()
    g = tiles(grads[0, 0])
    m = tiles(momentum[0])
    count = m.shape[1] // QUANTUM
    member = lax.axis_index("fsdp")
    place = jnp.stack([member, member ^ 1, member ^ 2, member ^ 3]).astype(jnp.int32)
    over_core = [(f, f ^ 1) for f in range(4)]
    over_z = [(f, f ^ 2) for f in range(4)]

    def core(x):
        return lax.ppermute(x, "fsdp", over_core)

    def link(x):
        return lax.ppermute(x, "fsdp", over_z)

    cells, later = tie(cast(place, g, 0, 1, 3), place)
    first = core(cells)
    cells, later = tie(cast(later, g, 1, count - 1, 3), later)
    rest = core(cells)
    mine = core(cast(later, g, 0, count, 1))
    pay0, band0 = encoded(place, g, first, 0, 1, 2, mats)
    pays, bands = encoded(place, g, rest, 1, count - 1, 2, mats)
    payloads = list(pay0) + list(pays)
    base, own_band = based(place, m, g, mine, 0, mats)
    other_band = jnp.concatenate([band0, bands], axis=0)

    groups = [[h * 16 + i for i in range(16)] for h in range(rep_count // 16)]
    both = jnp.stack([own_band, other_band], axis=1)
    met = lax.all_to_all(both, "rep", 0, 0, axis_index_groups=groups, tiled=True)
    part = jnp.sum(met, axis=0)
    names = ("rep", "fsdp")
    everyone = range(rep_count * 4)
    from_z = lax.ppermute(part[1], names, [(d, d ^ 2) for d in everyone])
    from_far = lax.ppermute(part[0], names, [(d, d ^ 64) for d in everyone])
    from_wrap = lax.ppermute(part[1], names, [(d, d ^ 66) for d in everyone])
    total = (part[0] + from_z) + (from_far + from_wrap)
    spread = jnp.broadcast_to(total[None], (16,) + total.shape)
    band_total = lax.all_to_all(spread, "rep", 0, 0, axis_index_groups=groups, tiled=True)
    update = updated(band_total, 1.0 / rep_count, m.shape, mats)

    arrived = []
    for k in range(count):
        if k >= 2:
            payloads[k], arrived[k - 2] = tie(payloads[k], arrived[k - 2])
        arrived.append(link(payloads[k]))
    out = base
    for k in range(count):
        out = decoded(arrived[k], out, k, mats)
    return (untiles(out, mat_count)[None], untiles(update, mat_count))


def solution(mesh):
    in_specs = (P("rep", "fsdp", None, None, None), P("rep", "fsdp", None, None))
    out_specs = (P("rep", "fsdp", None, None), P("fsdp", None, None))
    return jax.shard_map(
        per_device, mesh=mesh, in_specs=in_specs, out_specs=out_specs, check_vma=False
    )
```

```python
import functools
import math

import jax
import jax.numpy as jnp
import ml_dtypes
import numpy as np
from jax import lax
from jax.experimental import pallas as pl
from jax.experimental.pallas import tpu as pltpu
from jax.sharding import PartitionSpec as P

SPAN = 64
BAND = 16
LANES = 128
GROUP = 8
QUANTUM = 2 * GROUP
DECAY = 0.9
HIGH = SPAN - BAND
QUARTER = GROUP // 4 * BAND
PAYLOAD = QUANTUM * HIGH + 3 * SPAN
PLANE = 16
VMEM = 46 * 1024 * 1024


def dct(order):
    q = np.arange(order)[:, None]
    n = np.arange(order)[None, :]
    scale = np.where(q == 0, math.sqrt(1.0 / order), math.sqrt(2.0 / order))
    return scale * np.cos(math.pi * (2 * n + 1) * q / (2 * order))


def halves(a):
    high = a.astype(ml_dtypes.bfloat16)
    return high, (a - high.astype(np.float64)).astype(ml_dtypes.bfloat16)


def left(a):
    high, low = halves(a)
    return np.concatenate([high, low, high], axis=1)


def right(a):
    high, low = halves(a)
    return np.concatenate([high, low, high], axis=0)


def constants():
    t = dct(SPAN)
    lanes = np.kron(np.eye(8), t.T)
    coef = np.arange(512) % SPAN
    order = np.concatenate([np.flatnonzero(coef >= BAND), np.flatnonzero(coef < BAND)])
    lanes = lanes[:, order]
    kept, band = lanes[:, : 3 * LANES], lanes[:, 3 * LANES :]
    mats = dict(
        rows=left(t), rows_back=left(t.T), low=left(t[:BAND]), low_back=left(t[:BAND].T),
        lanes=right(lanes), kept_back=right(kept.T), band=right(band), band_back=right(band.T),
    )
    return {name: jnp.asarray(a) for name, a in mats.items()}


def split(x):
    high = x.astype(jnp.bfloat16)
    return high, (x - high.astype(jnp.float32)).astype(jnp.bfloat16)


def tall(x):
    high, low = split(x)
    return jnp.concatenate([high, high, low], axis=0)


def long(x):
    high, low = split(x)
    return jnp.concatenate([high, high, low], axis=1)


def dot(a, b):
    return jnp.dot(a, b, preferred_element_type=jnp.float32)


def beside(x):
    x = jnp.swapaxes(x, 0, 1)
    return [jnp.concatenate([x[4 * s + j] for j in range(4)], axis=1) for s in range(4)]


def apart(parts):
    x = jnp.stack([p[:, j * LANES : (j + 1) * LANES] for p in parts for j in range(4)], axis=0)
    return jnp.swapaxes(x, 0, 1)


def forward(x, rows):
    return [dot(rows, tall(part)) for part in beside(x)]


def back(parts, rows):
    return apart([dot(rows, tall(p)) for p in parts])


def bands_of(c):
    return [c[s * BAND : (s + 1) * BAND] for s in range(4)]


def rows_of(place, slot):
    return pl.ds(pl.multiple_of(place[slot] * SPAN, SPAN), SPAN)


def quantum(k):
    return pl.ds(k * QUANTUM, QUANTUM)


def load(constants, buffers, sems):
    copies = [pltpu.make_async_copy(c, b, sems.at[i]) for i, (c, b) in enumerate(zip(constants, buffers))]
    for copy in copies:
        copy.start()
    return copies


def cast_kernel(first, counts, slot, place, g_ref, *refs):
    outs, (held, cells, sems) = refs[: len(counts)], refs[len(counts) :]
    into, out = [], []
    for o, n in zip(outs, counts):
        for j in range(n):
            k = len(into)
            source = g_ref.at[rows_of(place, slot), quantum(first + k), :]
            into.append(pltpu.make_async_copy(source, held.at[k], sems.at[0, k]))
            out.append(pltpu.make_async_copy(cells.at[k], o.at[:, quantum(j), :], sems.at[1, k]))
            into[-1].start()
    for k in range(len(into)):
        into[k].wait()
        cells[k] = held[k].astype(jnp.float32)
        out[k].start()
    for copy in out:
        copy.wait()


def encode_kernel(first, count, skip, slot, place, g_ref, r_ref, rows, lanes, *refs):
    pay_ref, band_ref, g_buf, r_buf, pay_buf, band_buf, low_buf, rows_buf, lanes_buf, sems, const_sems = refs[-11:]
    high = QUANTUM * HIGH

    def into(k):
        yield pltpu.make_async_copy(g_ref.at[rows_of(place, slot), quantum(first + k), :], g_buf.at[k], sems.at[0, k])
        yield pltpu.make_async_copy(r_ref.at[:, quantum(skip + k), :], r_buf.at[k], sems.at[1, k])

    def out_high(k):
        at = pl.ds(0, high)
        return pltpu.make_async_copy(pay_buf.at[k, at], pay_ref.at[k, at], sems.at[2, k])

    def out_low(k):
        at = pl.ds(high, 3 * SPAN)
        yield pltpu.make_async_copy(pay_buf.at[k, at], pay_ref.at[k, at], sems.at[3, k])
        to = band_ref.at[pl.ds((first + k + PLANE // 2 - 2) % (PLANE // 2) * 2, 2), 1]
        yield pltpu.make_async_copy(band_buf.at[k], to, sems.at[4, k])

    for copy in into(0):
        copy.start()
    consts = load((rows, lanes), (rows_buf, lanes_buf), const_sems)
    for k in range(1, count):
        for copy in into(k):
            copy.start()
    consts[0].wait()

    def body(k, _):
        for copy in into(k):
            copy.wait()
        for s, c in enumerate(forward(g_buf[k].astype(jnp.float32) + r_buf[k], rows_buf[...])):
            low_buf[k, s * BAND : (s + 1) * BAND, :] = c[:BAND]
            for j in range(4):
                at = (4 * s + j) * HIGH
                pay_buf[k, at : at + HIGH, :] = c[BAND:, j * LANES : (j + 1) * LANES]
        out_high(k).start()
        return 0

    lax.fori_loop(0, count, body, 0)
    consts[1].wait()
    w = dot(long(low_buf[...].reshape(count * SPAN, 4 * LANES)), lanes_buf[...])
    for k in range(count):
        part = w[k * SPAN : (k + 1) * SPAN]
        for i in range(3):
            at = high + i * SPAN
            pay_buf[k, at : at + SPAN, :] = part[:, i * LANES : (i + 1) * LANES]
        band_buf[k] = part[:, 3 * LANES :].reshape(2, QUARTER, LANES)
        for copy in out_low(k):
            copy.start()
    for k in range(count):
        out_high(k).wait()
        for copy in out_low(k):
            copy.wait()


def base_kernel(counts, slot, place, m_ref, g_ref, *refs):
    received, refs = refs[: len(counts)], refs[len(counts) :]
    constants, refs = refs[:4], refs[5:]
    out_ref, band_ref, m_buf, g_buf, r_buf, out_buf, band_buf, low_buf = refs[:8]
    buffers, (sems, const_sems) = refs[8:12], refs[12:]
    total = sum(counts)
    where = [(r, j) for r, n in zip(received, counts) for j in range(n)]

    def into(k, r=None, j=0):
        yield pltpu.make_async_copy(m_ref.at[:, quantum(k), :], m_buf.at[k], sems.at[0, k])
        yield pltpu.make_async_copy(g_ref.at[rows_of(place, slot), quantum(k), :], g_buf.at[k], sems.at[1, k])
        r = received[0] if r is None else r
        yield pltpu.make_async_copy(r.at[:, quantum(j), :], r_buf.at[k], sems.at[2, k])

    def out(k):
        return pltpu.make_async_copy(out_buf.at[k], out_ref.at[:, quantum(k), :], sems.at[3, k])

    def out_band(k):
        return pltpu.make_async_copy(band_buf.at[k], band_ref.at[pl.ds(2 * k, 2), 0], sems.at[4, k])

    for copy in into(0, *where[0]):
        copy.start()
    consts = load(constants, buffers, const_sems)
    for k in range(1, total):
        for copy in into(k, *where[k]):
            copy.start()
    for copy in consts:
        copy.wait()
    low, low_back, band, band_back = buffers

    def body(k, _):
        for copy in into(k):
            copy.wait()
        cells = DECAY * m_buf[k] + (g_buf[k].astype(jnp.float32) + r_buf[k])
        m_buf[k] = cells
        for s, c in enumerate(forward(cells, low[...])):
            low_buf[k, s * BAND : (s + 1) * BAND, :] = c
        return 0

    lax.fori_loop(0, total, body, 0)
    b = dot(long(low_buf[...].reshape(total * SPAN, 4 * LANES)), band[...])
    band_buf[...] = b.reshape(total, 2, QUARTER, LANES)
    for k in range(total):
        out_band(k).start()
    low_buf[...] = dot(long(b), band_back[...]).reshape(total, SPAN, 4 * LANES)

    def body_back(k, _):
        out_buf[k] = m_buf[k] - back(bands_of(low_buf[k]), low_back[...])
        out(k).start()
        return 0

    lax.fori_loop(0, total, body_back, 0)
    for k in range(total):
        out(k).wait()
        out_band(k).wait()


def decode_kernel(first, count, pay_ref, rows_back, kept_back, base_ref, out_ref, *refs):
    pay_buf, base_buf, low_buf, rows_buf, kept_buf, sems, const_sems = refs
    at = QUANTUM * HIGH

    def into(k):
        yield pltpu.make_async_copy(pay_ref.at[k], pay_buf.at[k], sems.at[0, k])
        yield pltpu.make_async_copy(base_ref.at[:, quantum(first + k), :], base_buf.at[k], sems.at[1, k])

    def out(k):
        return pltpu.make_async_copy(base_buf.at[k], out_ref.at[:, quantum(first + k), :], sems.at[2, k])

    for k in range(count):
        for copy in into(k):
            copy.start()
    for copy in load((rows_back, kept_back), (rows_buf, kept_buf), const_sems):
        copy.wait()
    for k in range(count):
        for copy in into(k):
            copy.wait()
    kept = [
        jnp.concatenate([pay_buf[k, at + i * SPAN : at + (i + 1) * SPAN, :] for i in range(3)], axis=1)
        for k in range(count)
    ]
    low_buf[...] = dot(long(jnp.concatenate(kept, axis=0)), kept_buf[...]).reshape(count, SPAN, 4 * LANES)

    def body(k, _):
        parts = []
        for s, low in enumerate(bands_of(low_buf[k])):
            high = [pay_buf[k, (4 * s + j) * HIGH : (4 * s + j + 1) * HIGH, :] for j in range(4)]
            parts.append(jnp.concatenate([low, jnp.concatenate(high, axis=1)], axis=0))
        base_buf[k] = base_buf[k] + back(parts, rows_buf[...])
        out(k).start()
        return 0

    lax.fori_loop(0, count, body, 0)
    for k in range(count):
        out(k).wait()


def update_kernel(scale, count, band_ref, low_back, band_back, out_ref, band_buf, low_rows, back_buf, out_buf, low_buf, sems, const_sems):
    for copy in load((band_ref, low_back, band_back), (band_buf, low_rows, back_buf), const_sems):
        copy.wait()
    b = band_buf[...].reshape(count * SPAN, LANES) * scale
    low_buf[...] = dot(long(b), back_buf[...]).reshape(count, SPAN, 4 * LANES)

    def out(k):
        return pltpu.make_async_copy(out_buf.at[k], out_ref.at[:, quantum(k), :], sems.at[k])

    def body(k, _):
        out_buf[k] = back(bands_of(low_buf[k]), low_rows[...])
        out(k).start()
        return 0

    lax.fori_loop(0, count, body, 0)
    for k in range(count):
        out(k).wait()


ANY = pl.BlockSpec(memory_space=pl.ANY)
BANDS = jax.ShapeDtypeStruct((PLANE, 2, QUARTER, LANES), jnp.float32)


def call(kernel, place, operands, outs, scratch, aliases):
    scalars = [] if place is None else [place]
    return pl.pallas_call(
        kernel,
        grid_spec=pltpu.PrefetchScalarGridSpec(
            num_scalar_prefetch=len(scalars),
            grid=(),
            in_specs=[ANY] * len(operands),
            out_specs=[ANY] * len(outs),
            scratch_shapes=scratch,
        ),
        out_shape=outs,
        input_output_aliases=aliases,
        cost_estimate=pl.CostEstimate(flops=0, bytes_accessed=0, transcendentals=0),
        compiler_params=pltpu.CompilerParams(vmem_limit_bytes=VMEM),
    )(*scalars, *operands)


def floats(*shape):
    return jax.ShapeDtypeStruct(shape, jnp.float32)


def held(count, *dtypes):
    return [pltpu.VMEM((count, SPAN, QUANTUM, LANES), dtype) for dtype in dtypes]


def lows(count):
    return [pltpu.VMEM((count, SPAN, 4 * LANES), jnp.float32)]


def same(arrays):
    return [pltpu.VMEM(a.shape, a.dtype) for a in arrays]


def sems(*shape):
    return pltpu.SemaphoreType.DMA(shape)


def cast(place, g, first, counts, slot):
    n = sum(counts)
    return call(
        functools.partial(cast_kernel, first, counts, slot),
        place,
        [g],
        [floats(SPAN, c * QUANTUM, LANES) for c in counts],
        held(n, jnp.bfloat16, jnp.float32) + [sems(2, n)],
        {},
    )


def encoded(place, g, received, skip, first, count, slot, mats, bands=None):
    values = [mats["rows"], mats["lanes"]]
    more = [] if bands is None else [bands]
    return call(
        functools.partial(encode_kernel, first, count, skip, slot),
        place,
        [g, received, *values, *more],
        [floats(count, PAYLOAD, LANES), BANDS],
        held(count, jnp.bfloat16, jnp.float32)
        + [pltpu.VMEM((count, PAYLOAD, LANES), jnp.float32), pltpu.VMEM((count, 2, QUARTER, LANES), jnp.float32)]
        + lows(count)
        + same(values)
        + [sems(5, count), sems(2)],
        {5: 1} if more else {},
    )


def based(place, m, g, received, slot, mats, bands):
    values = [mats[name] for name in ("low", "low_back", "band", "band_back")]
    counts = [r.shape[1] // QUANTUM for r in received]
    n = sum(counts)
    return call(
        functools.partial(base_kernel, counts, slot),
        place,
        [m, g, *received, *values, bands],
        [floats(*m.shape), BANDS],
        held(n, jnp.float32, jnp.bfloat16, jnp.float32, jnp.float32)
        + [pltpu.VMEM((n, 2, QUARTER, LANES), jnp.float32)]
        + lows(n)
        + same(values)
        + [sems(5, n), sems(4)],
        {3 + len(received) + 4: 1},
    )


def decoded(payload, base, first, mats):
    values = [mats["rows_back"], mats["kept_back"]]
    count = payload.shape[0]
    return call(
        functools.partial(decode_kernel, first, count),
        None,
        [payload, *values, base],
        [floats(*base.shape)],
        [pltpu.VMEM((count, PAYLOAD, LANES), jnp.float32)]
        + held(count, jnp.float32)
        + lows(count)
        + same(values)
        + [sems(3, count), sems(2)],
        {3: 0},
    )[0]


def updated(band, scale, shape, mats):
    values = [mats["low_back"], mats["band_back"]]
    count = shape[1] // QUANTUM
    return call(
        functools.partial(update_kernel, scale, count),
        None,
        [band, *values],
        [floats(*shape)],
        same([band, *values]) + held(count, jnp.float32) + lows(count) + [sems(count), sems(3)],
        {},
    )[0]


def tiles(x):
    rows, mats, width = x.shape
    x = x.reshape(rows, mats, width // LANES, LANES).transpose(0, 2, 1, 3)
    return x.reshape(rows, mats * width // LANES, LANES)


def untiles(x, mats):
    rows, places, _ = x.shape
    x = x.reshape(rows, places // mats, mats, LANES).transpose(0, 2, 1, 3)
    return x.reshape(rows, mats, places // mats * LANES)


def tie(*arrays):
    return lax.optimization_barrier(arrays)


def per_device(grads, momentum):
    rep_count = lax.axis_size("rep")
    mat_count = grads.shape[3]
    mats = constants()
    g = tiles(grads[0, 0])
    m = tiles(momentum[0])
    count = m.shape[1] // QUANTUM
    member = lax.axis_index("fsdp")
    place = jnp.stack([member, member ^ 1, member ^ 2, member ^ 3]).astype(jnp.int32)
    over_core = [(f, f ^ 1) for f in range(4)]
    over_z = [(f, f ^ 2) for f in range(4)]

    def core(x):
        return lax.ppermute(x, "fsdp", over_core)

    def link(x):
        return lax.ppermute(x, "fsdp", over_z)

    (cells,) = cast(place, g, 0, (1,), 3)
    place1, cells = tie(place, cells)
    more, last = cast(place1, g, 1, (6, 1), 3)
    got, more = tie(core(cells), more)
    pay0, bands = encoded(place, g, got, 0, 0, 1, 2, mats)
    there0 = link(pay0)
    pay1, bands = encoded(place, g, core(more), 0, 1, 6, 2, mats, bands)
    place2, pay1 = tie(place1, pay1)
    mine = cast(place2, g, 0, (2, 2, 2, 2), 1)
    pay1, there0, *mine = tie(pay1, there0, *mine)
    there1 = link(pay1)
    pay2, bands = encoded(place, g, core(last), 0, 7, 1, 2, mats, bands)
    there2 = link(pay2)
    base, bands = based(place, m, g, [core(c) for c in mine], 0, mats, bands)

    groups = [[h * PLANE + i for i in range(PLANE)] for h in range(rep_count // PLANE)]
    met = lax.all_to_all(bands, "rep", 0, 0, axis_index_groups=groups, tiled=True)
    part = jnp.sum(met, axis=0)
    names = ("rep", "fsdp")
    own = part[0] + lax.ppermute(part[1], names, steps(rep_count, 1, 4, 2))
    other = part[1] + lax.ppermute(part[0], names, steps(rep_count, 1, -4, 2))
    total = own + lax.ppermute(other, names, steps(rep_count, 0, 4, 2))
    spread = jnp.broadcast_to(total[None], (PLANE,) + total.shape)
    band_total = lax.all_to_all(spread, "rep", 0, 0, axis_index_groups=groups, tiled=True)
    update = updated(band_total, 1.0 / rep_count, m.shape, mats)

    out = decoded(there0, base, 0, mats)
    there1, update = tie(there1, update)
    out = decoded(there1, out, 1, mats)
    there2, out = tie(there2, out)
    out = decoded(there2, out, 7, mats)
    return (untiles(out, mat_count)[None], untiles(update, mat_count))


def steps(rep_count, z_hi, plane, member):
    pairs = []
    for rep in range(rep_count):
        high, low = divmod(rep, PLANE)
        to = (high ^ z_hi) * PLANE + (low + plane) % PLANE
        pairs += [(rep * 4 + f, to * 4 + (f ^ member)) for f in range(4)]
    return pairs


def solution(mesh):
    in_specs = (P("rep", "fsdp", None, None, None), P("rep", "fsdp", None, None))
    out_specs = (P("rep", "fsdp", None, None), P("fsdp", None, None))
    return jax.shard_map(
        per_device, mesh=mesh, in_specs=in_specs, out_specs=out_specs, check_vma=False
    )
```

```python
import functools
import math

import jax
import jax.numpy as jnp
import ml_dtypes
import numpy as np
from jax import lax
from jax.experimental import pallas as pl
from jax.experimental.pallas import tpu as pltpu
from jax.sharding import PartitionSpec as P

SPAN = 64
BAND = 16
LANES = 128
GROUP = 8
QUANTUM = 2 * GROUP
DECAY = 0.9
HIGH = SPAN - BAND
QUARTER = GROUP // 4 * BAND
PAYLOAD = QUANTUM * HIGH + 3 * SPAN
SPLIT = 48
PLANE = 16
TURN = 4
MOST = 46


def dct(order):
    q = np.arange(order)[:, None]
    n = np.arange(order)[None, :]
    scale = np.where(q == 0, math.sqrt(1.0 / order), math.sqrt(2.0 / order))
    return scale * np.cos(math.pi * (2 * n + 1) * q / (2 * order))


def halves(a):
    high = a.astype(ml_dtypes.bfloat16)
    return high, (a - high.astype(np.float64)).astype(ml_dtypes.bfloat16)


def left(a):
    high, low = halves(a)
    return np.concatenate([high, low, high], axis=1)


def right(a):
    high, low = halves(a)
    return np.concatenate([high, low, high], axis=0)


def constants():
    t = dct(SPAN)
    lanes = np.kron(np.eye(8), t.T)
    coef = np.arange(512) % SPAN
    order = np.concatenate([np.flatnonzero(coef >= BAND), np.flatnonzero(coef < BAND)])
    lanes = lanes[:, order]
    kept, band = lanes[:, : 3 * LANES], lanes[:, 3 * LANES :]
    mats = dict(
        rows=left(t), rows_back=left(t.T), low=left(t[:BAND]), low_back=left(t[:BAND].T),
        lanes=right(lanes), kept_back=right(kept.T), band=right(band), band_back=right(band.T),
    )
    return {name: jnp.asarray(a) for name, a in mats.items()}


def split(x):
    high = x.astype(jnp.bfloat16)
    return high, (x - high.astype(jnp.float32)).astype(jnp.bfloat16)


def tall(x):
    high, low = split(x)
    return jnp.concatenate([high, high, low], axis=0)


def long(x):
    high, low = split(x)
    return jnp.concatenate([high, high, low], axis=1)


def dot(a, b):
    return jnp.dot(a, b, preferred_element_type=jnp.float32)


def beside(x):
    x = jnp.swapaxes(x, 0, 1)
    return [jnp.concatenate([x[4 * s + j] for j in range(4)], axis=1) for s in range(4)]


def apart(parts):
    x = jnp.stack([p[:, j * LANES : (j + 1) * LANES] for p in parts for j in range(4)], axis=0)
    return jnp.swapaxes(x, 0, 1)


def forward(x, rows):
    return [dot(rows, tall(part)) for part in beside(x)]


def back(parts, rows):
    return apart([dot(rows, tall(p)) for p in parts])


def bands_of(c):
    return [c[s * BAND : (s + 1) * BAND] for s in range(4)]


def rows_of(place, slot):
    return pl.ds(pl.multiple_of(place[slot] * SPAN, SPAN), SPAN)


def quantum(k):
    return pl.ds(k * QUANTUM, QUANTUM)


def band_at(k, shift):
    return pl.ds(lax.rem(2 * k + PLANE - shift, PLANE), 2)


def load(constants, buffers, sems):
    copies = [pltpu.make_async_copy(c, b, sems.at[i]) for i, (c, b) in enumerate(zip(constants, buffers))]
    for copy in copies:
        copy.start()
    return copies


def cast_kernel(first, counts, slot, place, g_ref, *refs):
    outs, (held, cells, sems) = refs[: len(counts)], refs[len(counts) :]
    into, out = [], []
    for o, n in zip(outs, counts):
        for j in range(n):
            k = len(into)
            source = g_ref.at[rows_of(place, slot), quantum(first + k), :]
            into.append(pltpu.make_async_copy(source, held.at[k], sems.at[0, k]))
            out.append(pltpu.make_async_copy(cells.at[k], o.at[:, quantum(j), :], sems.at[1, k]))
            into[-1].start()
    for k in range(len(into)):
        into[k].wait()
        cells[k] = held[k].astype(jnp.float32)
        out[k].start()
    for copy in out:
        copy.wait()


def encode_kernel(first, counts, slot, place, g_ref, r_ref, rows, lanes, *refs):
    pays, refs = refs[: len(counts)], refs[len(counts) :]
    band_ref, g_buf, r_buf, pay_buf, band_buf, low_buf, zero_buf, rows_buf, lanes_buf, sems, more_sems = refs
    high = QUANTUM * HIGH
    sent = sum(counts)
    count = sent + 1
    where = [(ref, j) for ref, n in zip(pays, counts) for j in range(n)]
    turn = place[5]

    def into(k):
        yield pltpu.make_async_copy(g_ref.at[rows_of(place, slot), quantum(first + k), :], g_buf.at[k], sems.at[0, k])
        yield pltpu.make_async_copy(r_ref.at[:, quantum(k), :], r_buf.at[k], sems.at[1, k])

    def out_high(k, ref, j):
        at = pl.ds(0, high)
        return pltpu.make_async_copy(pay_buf.at[k, at], ref.at[j, at], sems.at[2, k])

    def out_low(k, ref, j):
        at = pl.ds(high, 3 * SPAN)
        return pltpu.make_async_copy(pay_buf.at[k, at], ref.at[j, at], sems.at[3, k])

    def out_band(k):
        return pltpu.make_async_copy(band_buf.at[k], band_ref.at[band_at(first + k, turn)], sems.at[4, k])

    blank = pltpu.make_async_copy(zero_buf, band_ref.at[band_at(0, turn)], more_sems.at[2])
    for copy in into(0):
        copy.start()
    consts = load((rows, lanes), (rows_buf, lanes_buf), more_sems)
    for k in range(1, count):
        for copy in into(k):
            copy.start()
    zero_buf[...] = jnp.zeros_like(zero_buf)
    blank.start()
    consts[0].wait()

    def low_of(k, c, s):
        low_buf[k, s * BAND : (s + 1) * BAND, :] = c[:BAND]

    def cells_of(k):
        for copy in into(k):
            copy.wait()
        return g_buf[k].astype(jnp.float32) + r_buf[k]

    def body(k, _):
        for s, c in enumerate(forward(cells_of(k), rows_buf[...])):
            low_of(k, c, s)
            for j in range(4):
                at = (4 * s + j) * HIGH
                pay_buf[k, at : at + HIGH, :] = c[BAND:, j * LANES : (j + 1) * LANES]
        for i, ref in enumerate(pays):
            start = sum(counts[:i])

            @pl.when((k >= start) & (k < start + counts[i]))
            def _():
                out_high(k, ref, k - start).start()

        return 0

    lax.fori_loop(0, sent, body, 0)
    for k in range(sent, count):
        for s, c in enumerate(forward(cells_of(k), rows_buf[:BAND, :])):
            low_of(k, c, s)
    consts[1].wait()
    w = dot(long(low_buf[...].reshape(count * SPAN, 4 * LANES)), lanes_buf[...])
    for k in range(count):
        part = w[k * SPAN : (k + 1) * SPAN]
        if k < sent:
            for i in range(3):
                at = high + i * SPAN
                pay_buf[k, at : at + SPAN, :] = part[:, i * LANES : (i + 1) * LANES]
            out_low(k, *where[k]).start()
        band_buf[k] = part[:, 3 * LANES :].reshape(2, QUARTER, LANES)
        out_band(k).start()
    for k in range(count):
        if k < sent:
            out_high(k, *where[k]).wait()
            out_low(k, *where[k]).wait()
        out_band(k).wait()
    blank.wait()


def base_kernel(counts, mine, theirs, place, m_ref, g_ref, early_ref, theirs_ref, *refs):
    received, refs = refs[: len(counts)], refs[len(counts) :]
    constants, refs = refs[:4], refs[4:]
    out_ref, top_ref, bottom_ref, band_ref = refs[:4]
    m_buf, g_buf, r_buf, out_buf, band_buf, low_buf, early_buf = refs[4:11]
    buffers, (sems, const_sems, more_sems) = refs[11:15], refs[15:]
    total = sum(counts)
    where = [(r, j) for r, n in zip(received, counts) for j in range(n)] + [(theirs_ref, theirs_ref.shape[1] // QUANTUM - 1)]
    split = top_ref.shape[0]

    def into(k, r=None, j=0):
        r, slot, at = (received[0], mine, k) if r is None else (r, theirs if r is theirs_ref else mine, min(k, total - 1))
        yield pltpu.make_async_copy(g_ref.at[rows_of(place, slot), quantum(at), :], g_buf.at[k], sems.at[0, k])
        yield pltpu.make_async_copy(r.at[:, quantum(j), :], r_buf.at[k], sems.at[1, k])

    def moment(k):
        return pltpu.make_async_copy(m_ref.at[:, quantum(k), :], m_buf.at[k], sems.at[2, k])

    def out(k):
        return pltpu.make_async_copy(out_buf.at[k], out_ref.at[:, quantum(k), :], sems.at[3, k])

    def out_band(k):
        return pltpu.make_async_copy(band_buf.at[k], band_ref.at[band_at(k, place[4])], sems.at[4, k])

    def out_last():
        yield pltpu.make_async_copy(out_buf.at[total, pl.ds(0, split)], top_ref, more_sems.at[0])
        yield pltpu.make_async_copy(out_buf.at[total, pl.ds(split, SPAN - split)], bottom_ref, more_sems.at[1])

    early = pltpu.make_async_copy(early_ref, early_buf, more_sems.at[2])
    for copy in (*into(0, *where[0]), moment(0), early):
        copy.start()
    consts = load(constants, buffers, const_sems)
    for k in range(1, total + 1):
        for copy in into(k, *where[k]):
            copy.start()
        if k < total:
            moment(k).start()
    for copy in consts:
        copy.wait()
    low, low_back, band, band_back = buffers

    def cells_of(k, add):
        for copy in into(k, *(where[k] if isinstance(k, int) else ())):
            copy.wait()
        cells = add(g_buf[k].astype(jnp.float32) + r_buf[k])
        m_buf[k] = cells
        for s, c in enumerate(forward(cells, low[...])):
            low_buf[k, s * BAND : (s + 1) * BAND, :] = c

    def own_cells(k, more=None):
        moment(k).wait()
        decayed = DECAY * m_buf[k]
        cells_of(k, lambda x: decayed + (x if more is None else x + more))

    def body(k, _):
        own_cells(k)
        return 0

    early.wait()
    own_cells(0, early_buf[...])
    lax.fori_loop(1, total, body, 0)
    cells_of(total, lambda x: x)
    b = dot(long(low_buf[...].reshape((total + 1) * SPAN, 4 * LANES)), band[...])
    band_buf[...] = b.reshape(total + 1, 2, QUARTER, LANES)
    for k in range(total):
        out_band(k).start()
    low_buf[...] = dot(long(b), band_back[...]).reshape(total + 1, SPAN, 4 * LANES)

    def without_band(k):
        out_buf[k] = m_buf[k] - back(bands_of(low_buf[k]), low_back[...])

    def body_back(k, _):
        without_band(k)
        out(k).start()
        return 0

    without_band(total)
    for copy in out_last():
        copy.start()
    lax.fori_loop(0, total, body_back, 0)
    for k in range(total):
        out(k).wait()
        out_band(k).wait()
    for copy in out_last():
        copy.wait()


def decode_kernel(first, count, pay_ref, rows_back, kept_back, base_ref, out_ref, *refs):
    pay_buf, base_buf, low_buf, rows_buf, kept_buf, sems, const_sems = refs
    at = QUANTUM * HIGH

    def into(k):
        yield pltpu.make_async_copy(pay_ref.at[k], pay_buf.at[k], sems.at[0, k])
        yield pltpu.make_async_copy(base_ref.at[:, quantum(first + k), :], base_buf.at[k], sems.at[1, k])

    def out(k):
        return pltpu.make_async_copy(base_buf.at[k], out_ref.at[:, quantum(first + k), :], sems.at[2, k])

    for k in range(count):
        for copy in into(k):
            copy.start()
    for copy in load((rows_back, kept_back), (rows_buf, kept_buf), const_sems):
        copy.wait()
    for k in range(count):
        for copy in into(k):
            copy.wait()
    kept = [
        jnp.concatenate([pay_buf[k, at + i * SPAN : at + (i + 1) * SPAN, :] for i in range(3)], axis=1)
        for k in range(count)
    ]
    low_buf[...] = dot(long(jnp.concatenate(kept, axis=0)), kept_buf[...]).reshape(count, SPAN, 4 * LANES)

    def body(k, _):
        parts = []
        for s, low in enumerate(bands_of(low_buf[k])):
            high = [pay_buf[k, (4 * s + j) * HIGH : (4 * s + j + 1) * HIGH, :] for j in range(4)]
            parts.append(jnp.concatenate([low, jnp.concatenate(high, axis=1)], axis=0))
        base_buf[k] = base_buf[k] + back(parts, rows_buf[...])
        out(k).start()
        return 0

    lax.fori_loop(0, count, body, 0)
    for k in range(count):
        out(k).wait()


def add_kernel(first, row, there_ref, base_ref, out_ref, there_buf, base_buf, sems):
    at = (pl.ds(row, there_ref.shape[0]), quantum(first))
    into = [
        pltpu.make_async_copy(there_ref, there_buf, sems.at[0]),
        pltpu.make_async_copy(base_ref.at[at], base_buf, sems.at[1]),
    ]
    for copy in into:
        copy.start()
    for copy in into:
        copy.wait()
    base_buf[...] += there_buf[...]
    out = pltpu.make_async_copy(base_buf, out_ref.at[at], sems.at[2])
    out.start()
    out.wait()


def update_kernel(scale, count, place, band_ref, low_back, band_back, out_ref, band_buf, low_rows, back_buf, out_buf, low_buf, sems, const_sems):
    for copy in load((band_ref, low_back, band_back), (band_buf, low_rows, back_buf), const_sems):
        copy.wait()
    b = band_buf[...].reshape(count * SPAN, LANES) * scale
    low_buf[...] = dot(long(b), back_buf[...]).reshape(count, SPAN, 4 * LANES)

    def out(k):
        return pltpu.make_async_copy(out_buf.at[k], out_ref.at[:, quantum(k), :], sems.at[k])

    def body(k, _):
        turned = lax.rem(k + count - lax.div(place[4], 2), count)
        out_buf[k] = back(bands_of(low_buf[turned]), low_rows[...])
        out(k).start()
        return 0

    lax.fori_loop(0, count, body, 0)
    for k in range(count):
        out(k).wait()


ANY = pl.BlockSpec(memory_space=pl.ANY)
BANDS = jax.ShapeDtypeStruct((PLANE, QUARTER, LANES), jnp.float32)


def call(kernel, place, operands, outs, scratch, aliases, vmem):
    scalars = [] if place is None else [place]
    return pl.pallas_call(
        kernel,
        grid_spec=pltpu.PrefetchScalarGridSpec(
            num_scalar_prefetch=len(scalars),
            grid=(),
            in_specs=[ANY] * len(operands),
            out_specs=[ANY] * len(outs),
            scratch_shapes=scratch,
        ),
        out_shape=outs,
        input_output_aliases=aliases,
        cost_estimate=pl.CostEstimate(flops=0, bytes_accessed=0, transcendentals=0),
        compiler_params=pltpu.CompilerParams(vmem_limit_bytes=vmem * 1024 * 1024),
    )(*scalars, *operands)


def floats(*shape):
    return jax.ShapeDtypeStruct(shape, jnp.float32)


def held(count, *dtypes):
    return [pltpu.VMEM((count, SPAN, QUANTUM, LANES), dtype) for dtype in dtypes]


def lows(count):
    return [pltpu.VMEM((count, SPAN, 4 * LANES), jnp.float32)]


def same(arrays):
    return [pltpu.VMEM(a.shape, a.dtype) for a in arrays]


def sems(*shape):
    return pltpu.SemaphoreType.DMA(shape)


def cast(place, g, first, counts, slot):
    n = sum(counts)
    return call(
        functools.partial(cast_kernel, first, counts, slot),
        place,
        [g],
        [floats(SPAN, c * QUANTUM, LANES) for c in counts],
        held(n, jnp.bfloat16, jnp.float32) + [sems(2, n)],
        {},
        MOST,
    )


def encoded(place, g, received, first, counts, slot, mats):
    values = [mats["rows"], mats["lanes"]]
    sent = sum(counts)
    return call(
        functools.partial(encode_kernel, first, counts, slot),
        place,
        [g, received, *values],
        [floats(n, PAYLOAD, LANES) for n in counts] + [BANDS],
        held(sent + 1, jnp.bfloat16, jnp.float32)
        + [pltpu.VMEM((sent, PAYLOAD, LANES), jnp.float32), pltpu.VMEM((sent + 1, 2, QUARTER, LANES), jnp.float32)]
        + lows(sent + 1)
        + [pltpu.VMEM((2, QUARTER, LANES), jnp.float32)]
        + same(values)
        + [sems(5, sent + 1), sems(3)],
        {},
        MOST,
    )


def based(place, m, g, early, other, received, mine, theirs, mats):
    values = [mats[name] for name in ("low", "low_back", "band", "band_back")]
    counts = [r.shape[1] // QUANTUM for r in received]
    n = sum(counts) + 1
    return call(
        functools.partial(base_kernel, counts, mine, theirs),
        place,
        [m, g, early, other, *received, *values],
        [floats(*m.shape), floats(SPLIT, QUANTUM, LANES), floats(SPAN - SPLIT, QUANTUM, LANES), BANDS],
        held(n, jnp.float32, jnp.bfloat16, jnp.float32, jnp.float32)
        + [pltpu.VMEM((n, 2, QUARTER, LANES), jnp.float32)]
        + lows(n)
        + [pltpu.VMEM((SPAN, QUANTUM, LANES), jnp.float32)]
        + same(values)
        + [sems(5, n), sems(4), sems(3)],
        {},
        MOST,
    )


def added(there, base, first, row, mats):
    return call(
        functools.partial(add_kernel, first, row),
        None,
        [there, base],
        [floats(*base.shape)],
        same([there, there]) + [sems(3)],
        {1: 0},
        MOST,
    )[0]


def decoded(payload, base, first, mats):
    values = [mats["rows_back"], mats["kept_back"]]
    count = payload.shape[0]
    return call(
        functools.partial(decode_kernel, first, count),
        None,
        [payload, *values, base],
        [floats(*base.shape)],
        [pltpu.VMEM((count, PAYLOAD, LANES), jnp.float32)]
        + held(count, jnp.float32)
        + lows(count)
        + same(values)
        + [sems(3, count), sems(2)],
        {3: 0},
        MOST,
    )[0]


def updated(place, band, scale, shape, mats):
    values = [mats["low_back"], mats["band_back"]]
    count = shape[1] // QUANTUM
    return call(
        functools.partial(update_kernel, scale, count),
        place,
        [band, *values],
        [floats(*shape)],
        same([band, *values]) + held(count, jnp.float32) + lows(count) + [sems(count), sems(3)],
        {},
        MOST,
    )[0]


def tiles(x):
    rows, mats, width = x.shape
    x = x.reshape(rows, mats, width // LANES, LANES).transpose(0, 2, 1, 3)
    return x.reshape(rows, mats * width // LANES, LANES)


def untiles(x, mats):
    rows, places, _ = x.shape
    x = x.reshape(rows, places // mats, mats, LANES).transpose(0, 2, 1, 3)
    return x.reshape(rows, mats, places // mats * LANES)


def tie(*arrays):
    return lax.optimization_barrier(arrays)


def per_device(grads, momentum):
    rep_count = lax.axis_size("rep")
    mat_count = grads.shape[3]
    mats = constants()
    g = tiles(grads[0, 0])
    m = tiles(momentum[0])
    count = m.shape[1] // QUANTUM
    member = lax.axis_index("fsdp")
    turn = lax.axis_index("rep") // PLANE * TURN
    place = jnp.stack([member, member ^ 1, member ^ 2, member ^ 3, turn, TURN - turn]).astype(jnp.int32)
    over_core = [(f, f ^ 1) for f in range(4)]
    over_z = [(f, f ^ 2) for f in range(4)]

    def core(x):
        return lax.ppermute(x, "fsdp", over_core)

    def link(x):
        return lax.ppermute(x, "fsdp", over_z)

    def head(slot):
        return lax.dynamic_slice(g, (place[slot] * SPAN, 0, 0), (SPAN, QUANTUM, LANES)).astype(jnp.float32)

    place1, cells = tie(place, head(3))
    (more,) = cast(place1, g, 1, (count - 1,), 3)
    got, more = tie(core(cells), more)
    cells = head(2) + got
    early = link(cells)
    place2, cells = tie(place1, cells)
    mine = cast(place2, g, 0, (2, 2, 2), 1)
    got, *mine = tie(core(more), *mine)
    *pays, other_band = encoded(place, g, got, 1, (4, 2), 2, mats)
    theres = [link(pay) for pay in pays]
    names = ("rep", "fsdp")
    wrapped = lax.ppermute(other_band, names, steps(rep_count, 0, 2))
    place3, early, _ = tie(place2, early, pays[0])
    mine = [core(c) for c in [*mine, *cast(place3, g, 6, (2,), 1)]]
    base, top, bottom, own_band = based(place, m, g, early, got, mine, 0, 2, mats)
    top, bottom = link(top), link(bottom)

    groups = [[h * PLANE + i for i in range(PLANE)] for h in range(rep_count // PLANE)]
    met = lax.all_to_all(own_band + wrapped, "rep", 0, 0, axis_index_groups=groups, tiled=True)
    part = jnp.sum(met.reshape(PLANE, QUARTER, LANES), axis=0)
    total = part + lax.ppermute(part, names, steps(rep_count, TURN, 0))
    spread = jnp.broadcast_to(total[None], (PLANE,) + total.shape)
    band_total = lax.all_to_all(spread, "rep", 0, 0, axis_index_groups=groups, tiled=True)
    update = updated(place, band_total, 1.0 / rep_count, m.shape, mats)

    theres[1], update = tie(theres[1], update)
    out, first = base, 1
    for there in theres:
        there, out = tie(there, out)
        out = decoded(there, out, first, mats)
        first += there.shape[0]
    top, out = tie(top, out)
    out = added(top, out, count - 1, 0, mats)
    bottom, out = tie(bottom, out)
    out = added(bottom, out, count - 1, SPLIT, mats)
    return (untiles(out, mat_count)[None], untiles(update, mat_count))


def steps(rep_count, turn, member):
    pairs = []
    for rep in range(rep_count):
        high, low = divmod(rep, PLANE)
        to = (high ^ 1) * PLANE + (low + (turn if high else PLANE - turn)) % PLANE
        pairs += [(rep * 4 + f, to * 4 + (f ^ member)) for f in range(4)]
    return pairs


def solution(mesh):
    in_specs = (P("rep", "fsdp", None, None, None), P("rep", "fsdp", None, None))
    out_specs = (P("rep", "fsdp", None, None), P("fsdp", None, None))
    return jax.shard_map(
        per_device, mesh=mesh, in_specs=in_specs, out_specs=out_specs, check_vma=False
    )
```

```python
import functools
import math

import jax
import jax.numpy as jnp
import ml_dtypes
import numpy as np
from jax import lax
from jax.experimental import pallas as pl
from jax.experimental.pallas import tpu as pltpu
from jax.sharding import PartitionSpec as P

SPAN = 64
BAND = 16
LANES = 128
GROUP = 8
QUANTUM = 2 * GROUP
DECAY = 0.9
HIGH = SPAN - BAND
QUARTER = GROUP // 4 * BAND
PAYLOAD = QUANTUM * HIGH + 3 * SPAN
SECOND = 4
SPLIT = 48
PLANE = 16
TURN = 4
MOST = 46


def dct(order):
    q = np.arange(order)[:, None]
    n = np.arange(order)[None, :]
    scale = np.where(q == 0, math.sqrt(1.0 / order), math.sqrt(2.0 / order))
    return scale * np.cos(math.pi * (2 * n + 1) * q / (2 * order))


def halves(a):
    high = a.astype(ml_dtypes.bfloat16)
    return high, (a - high.astype(np.float64)).astype(ml_dtypes.bfloat16)


def left(a):
    high, low = halves(a)
    return np.concatenate([high, low, high], axis=1)


def right(a):
    high, low = halves(a)
    return np.concatenate([high, low, high], axis=0)


def constants():
    t = dct(SPAN)
    lanes = np.kron(np.eye(8), t.T)
    coef = np.arange(512) % SPAN
    order = np.concatenate([np.flatnonzero(coef >= BAND), np.flatnonzero(coef < BAND)])
    lanes = lanes[:, order]
    kept, band = lanes[:, : 3 * LANES], lanes[:, 3 * LANES :]
    mats = dict(
        rows=left(t), rows_back=left(t.T), low=left(t[:BAND]), low_back=left(t[:BAND].T),
        lanes=right(lanes), kept_back=right(kept.T), band=right(band), band_back=right(band.T),
    )
    return {name: jnp.asarray(a) for name, a in mats.items()}


def split(x):
    high = x.astype(jnp.bfloat16)
    return high, (x - high.astype(jnp.float32)).astype(jnp.bfloat16)


def tall(x):
    high, low = split(x)
    return jnp.concatenate([high, high, low], axis=0)


def long(x):
    high, low = split(x)
    return jnp.concatenate([high, high, low], axis=1)


def dot(a, b):
    return jnp.dot(a, b, preferred_element_type=jnp.float32)


def beside(x):
    x = jnp.swapaxes(x, 0, 1)
    return [jnp.concatenate([x[4 * s + j] for j in range(4)], axis=1) for s in range(4)]


def apart(parts):
    x = jnp.stack([p[:, j * LANES : (j + 1) * LANES] for p in parts for j in range(4)], axis=0)
    return jnp.swapaxes(x, 0, 1)


def forward(x, rows):
    return [dot(rows, tall(part)) for part in beside(x)]


def back(parts, rows):
    return apart([dot(rows, tall(p)) for p in parts])


def bands_of(c):
    return [c[s * BAND : (s + 1) * BAND] for s in range(4)]


def rows_of(place, slot):
    return pl.ds(pl.multiple_of(place[slot] * SPAN, SPAN), SPAN)


def quantum(k):
    return pl.ds(k * QUANTUM, QUANTUM)


def band_at(k, shift):
    return pl.ds(lax.rem(2 * k + PLANE - shift, PLANE), 2)


def load(constants, buffers, sems):
    copies = [pltpu.make_async_copy(c, b, sems.at[i]) for i, (c, b) in enumerate(zip(constants, buffers))]
    for copy in copies:
        copy.start()
    return copies


def cast_kernel(wanted, place, g_ref, *refs):
    outs, (held, cells, sems) = refs[: len(wanted)], refs[len(wanted) :]
    into, out = [], []
    for o, (slot, first, n) in zip(outs, wanted):
        for j in range(n):
            k = len(into)
            source = g_ref.at[rows_of(place, slot), quantum(first + j), :]
            into.append(pltpu.make_async_copy(source, held.at[k], sems.at[0, k]))
            out.append(pltpu.make_async_copy(cells.at[k], o.at[:, quantum(j), :], sems.at[1, k]))
            into[-1].start()
    for k in range(len(into)):
        into[k].wait()
        cells[k] = held[k].astype(jnp.float32)
        out[k].start()
    for copy in out:
        copy.wait()


def encode_kernel(first, counts, extra, slot, received, place, g_ref, *refs):
    come = [(ref, j) for ref, n in zip(refs, received) for j in range(n)]
    rows, lanes, *refs = refs[len(received) :]
    refs = refs[extra:]
    pays, refs = refs[: len(counts)], refs[len(counts) :]
    band_ref, g_buf, r_buf, pay_buf, band_buf, low_buf, zero_buf, rows_buf, lanes_buf, sems, more_sems = refs
    high = QUANTUM * HIGH
    sent = sum(counts)
    count = sent + extra
    where = [(ref, j) for ref, n in zip(pays, counts) for j in range(n)]
    turn = place[5]

    def into(k, ref=None, j=0):
        ref = come[0][0] if ref is None else ref
        yield pltpu.make_async_copy(g_ref.at[rows_of(place, slot), quantum(first + k), :], g_buf.at[k], sems.at[0, k])
        yield pltpu.make_async_copy(ref.at[:, quantum(j), :], r_buf.at[k], sems.at[1, k])

    def out_high(k, ref, j):
        at = pl.ds(0, high)
        return pltpu.make_async_copy(pay_buf.at[k, at], ref.at[j, at], sems.at[2, k])

    def out_low(k, ref, j):
        at = pl.ds(high, 3 * SPAN)
        return pltpu.make_async_copy(pay_buf.at[k, at], ref.at[j, at], sems.at[3, k])

    def out_band(k):
        return pltpu.make_async_copy(band_buf.at[k], band_ref.at[band_at(first + k, turn)], sems.at[4, k])

    if not extra:
        blank = pltpu.make_async_copy(zero_buf, band_ref.at[band_at(0, turn)], more_sems.at[2])
    for copy in into(0, *come[0]):
        copy.start()
    consts = load((rows, lanes), (rows_buf, lanes_buf), more_sems)
    for k in range(1, count):
        for copy in into(k, *come[k]):
            copy.start()
    if not extra:
        zero_buf[...] = jnp.zeros_like(zero_buf)
        blank.start()
    consts[0].wait()

    def low_of(k, c, s):
        low_buf[k, s * BAND : (s + 1) * BAND, :] = c[:BAND]

    def cells_of(k):
        for copy in into(k):
            copy.wait()
        return g_buf[k].astype(jnp.float32) + r_buf[k]

    def body(k, _):
        for s, c in enumerate(forward(cells_of(k), rows_buf[...])):
            low_of(k, c, s)
            for j in range(4):
                at = (4 * s + j) * HIGH
                pay_buf[k, at : at + HIGH, :] = c[BAND:, j * LANES : (j + 1) * LANES]
        for i, ref in enumerate(pays):
            start = sum(counts[:i])

            @pl.when((k >= start) & (k < start + counts[i]))
            def _():
                out_high(k, ref, k - start).start()

        return 0

    lax.fori_loop(0, sent, body, 0)
    for k in range(sent, count):
        for s, c in enumerate(forward(cells_of(k), rows_buf[:BAND, :])):
            low_of(k, c, s)
    consts[1].wait()
    w = dot(long(low_buf[...].reshape(count * SPAN, 4 * LANES)), lanes_buf[...])
    for k in range(count):
        part = w[k * SPAN : (k + 1) * SPAN]
        if k < sent:
            for i in range(3):
                at = high + i * SPAN
                pay_buf[k, at : at + SPAN, :] = part[:, i * LANES : (i + 1) * LANES]
            out_low(k, *where[k]).start()
        band_buf[k] = part[:, 3 * LANES :].reshape(2, QUARTER, LANES)
        out_band(k).start()
    for k in range(count):
        if k < sent:
            out_high(k, *where[k]).wait()
            out_low(k, *where[k]).wait()
        out_band(k).wait()
    if not extra:
        blank.wait()


def moment_kernel(counts, slot, place, m_ref, g_ref, early_ref, *refs):
    received, refs = refs[: len(counts)], refs[len(counts) :]
    constants, refs = refs[:2], refs[2:]
    cells_ref, band_ref, m_buf, g_buf, r_buf, band_buf, low_buf, early_buf = refs[:8]
    buffers, (sems, more_sems) = refs[8:10], refs[10:]
    total = sum(counts)
    where = [(r, j) for r, n in zip(received, counts) for j in range(n)]

    def into(k, r=None, j=0):
        r = received[0] if r is None else r
        yield pltpu.make_async_copy(g_ref.at[rows_of(place, slot), quantum(k), :], g_buf.at[k], sems.at[0, k])
        yield pltpu.make_async_copy(r.at[:, quantum(j), :], r_buf.at[k], sems.at[1, k])
        yield pltpu.make_async_copy(m_ref.at[:, quantum(k), :], m_buf.at[k], sems.at[2, k])

    def out(k):
        return pltpu.make_async_copy(m_buf.at[k], cells_ref.at[:, quantum(k), :], sems.at[3, k])

    def out_band(k):
        return pltpu.make_async_copy(band_buf.at[k], band_ref.at[band_at(k, place[4])], sems.at[4, k])

    early = pltpu.make_async_copy(early_ref, early_buf, more_sems.at[2])
    for copy in (*into(0, *where[0]), early):
        copy.start()
    consts = load(constants, buffers, more_sems)
    for k in range(1, total):
        for copy in into(k, *where[k]):
            copy.start()
    for copy in consts:
        copy.wait()
    low, band = buffers

    def cells_of(k, more=None):
        for copy in into(k):
            copy.wait()
        cells = DECAY * m_buf[k] + (g_buf[k].astype(jnp.float32) + r_buf[k])
        if more is not None:
            cells = cells + more
        m_buf[k] = cells
        out(k).start()
        for s, c in enumerate(forward(cells, low[...])):
            low_buf[k, s * BAND : (s + 1) * BAND, :] = c

    def body(k, _):
        cells_of(k)
        return 0

    early.wait()
    cells_of(0, early_buf[...])
    lax.fori_loop(1, total, body, 0)
    b = dot(long(low_buf[...].reshape(total * SPAN, 4 * LANES)), band[...])
    band_buf[...] = b.reshape(total, 2, QUARTER, LANES)
    for k in range(total):
        out_band(k).start()
    for k in range(total):
        out(k).wait()
        out_band(k).wait()


def rest_kernel(slot, place, cells_ref, bands_ref, g_ref, r_ref, *refs):
    constants, refs = refs[:4], refs[4:]
    out_ref, last_ref, top_ref, bottom_ref = refs[:4]
    cells_buf, band_buf, low_buf, g_buf, r_buf, theirs_buf = refs[4:10]
    buffers, (sems, more_sems) = refs[10:14], refs[14:]
    total = cells_buf.shape[0]
    split = top_ref.shape[0]

    def into(k):
        return pltpu.make_async_copy(cells_ref.at[:, quantum(k), :], cells_buf.at[k], sems.at[0, k])

    def out(k):
        return pltpu.make_async_copy(cells_buf.at[k], out_ref.at[:, quantum(k), :], sems.at[1, k])

    def out_last():
        yield pltpu.make_async_copy(cells_buf.at[total - 1], last_ref, more_sems.at[4])
        yield pltpu.make_async_copy(theirs_buf.at[pl.ds(0, split)], top_ref, more_sems.at[5])
        yield pltpu.make_async_copy(theirs_buf.at[pl.ds(split, SPAN - split)], bottom_ref, more_sems.at[6])

    theirs = [
        pltpu.make_async_copy(g_ref.at[rows_of(place, slot), quantum(total - 1), :], g_buf, more_sems.at[7]),
        pltpu.make_async_copy(r_ref.at[:, quantum(r_ref.shape[1] // QUANTUM - 1), :], r_buf, more_sems.at[8]),
        pltpu.make_async_copy(bands_ref, band_buf, more_sems.at[9]),
    ]
    for copy in theirs:
        copy.start()
    consts = load(constants, buffers, more_sems)
    for k in range(total):
        into(k).start()
    for copy in (*theirs, *consts):
        copy.wait()
    low, low_back, band, band_back = buffers

    theirs_buf[...] = g_buf[...].astype(jnp.float32) + r_buf[...]
    c = jnp.concatenate(forward(theirs_buf[...], low[...]), axis=0)
    theirs_band = dot(long(c), band[...])
    b = jnp.concatenate([band_buf[...].reshape(total * SPAN, LANES), theirs_band], axis=0)
    low_buf[...] = dot(long(b), band_back[...]).reshape(total + 1, SPAN, 4 * LANES)
    theirs_buf[...] = theirs_buf[...] - back(bands_of(low_buf[total]), low_back[...])

    def body(k, _):
        into(k).wait()
        turned = lax.rem(k + total - lax.div(place[4], 2), total)
        cells_buf[k] = cells_buf[k] - back(bands_of(low_buf[turned]), low_back[...])

        @pl.when(k < total - 1)
        def _():
            out(k).start()

        return 0

    lax.fori_loop(0, total, body, 0)
    for copy in out_last():
        copy.start()
    for k in range(total - 1):
        out(k).wait()
    for copy in out_last():
        copy.wait()


def decode_kernel(first, count, pay_ref, rows_back, kept_back, base_ref, out_ref, *refs):
    pay_buf, base_buf, low_buf, rows_buf, kept_buf, sems, const_sems = refs
    at = QUANTUM * HIGH

    def into(k):
        yield pltpu.make_async_copy(pay_ref.at[k], pay_buf.at[k], sems.at[0, k])
        yield pltpu.make_async_copy(base_ref.at[:, quantum(first + k), :], base_buf.at[k], sems.at[1, k])

    def out(k):
        return pltpu.make_async_copy(base_buf.at[k], out_ref.at[:, quantum(first + k), :], sems.at[2, k])

    for k in range(count):
        for copy in into(k):
            copy.start()
    for copy in load((rows_back, kept_back), (rows_buf, kept_buf), const_sems):
        copy.wait()
    for k in range(count):
        for copy in into(k):
            copy.wait()
    kept = [
        jnp.concatenate([pay_buf[k, at + i * SPAN : at + (i + 1) * SPAN, :] for i in range(3)], axis=1)
        for k in range(count)
    ]
    low_buf[...] = dot(long(jnp.concatenate(kept, axis=0)), kept_buf[...]).reshape(count, SPAN, 4 * LANES)

    def body(k, _):
        parts = []
        for s, low in enumerate(bands_of(low_buf[k])):
            high = [pay_buf[k, (4 * s + j) * HIGH : (4 * s + j + 1) * HIGH, :] for j in range(4)]
            parts.append(jnp.concatenate([low, jnp.concatenate(high, axis=1)], axis=0))
        base_buf[k] = base_buf[k] + back(parts, rows_buf[...])
        out(k).start()
        return 0

    lax.fori_loop(0, count, body, 0)
    for k in range(count):
        out(k).wait()


def add_kernel(first, row, there_ref, last_ref, base_ref, out_ref, there_buf, last_buf, sems):
    rows = pl.ds(row, there_ref.shape[0])
    into = [
        pltpu.make_async_copy(there_ref, there_buf, sems.at[0]),
        pltpu.make_async_copy(last_ref.at[rows], last_buf, sems.at[1]),
    ]
    for copy in into:
        copy.start()
    for copy in into:
        copy.wait()
    last_buf[...] += there_buf[...]
    out = pltpu.make_async_copy(last_buf, out_ref.at[rows, quantum(first)], sems.at[2])
    out.start()
    out.wait()


def update_kernel(scale, count, place, band_ref, low_back, band_back, out_ref, band_buf, low_rows, back_buf, out_buf, low_buf, sems, const_sems):
    for copy in load((band_ref, low_back, band_back), (band_buf, low_rows, back_buf), const_sems):
        copy.wait()
    b = band_buf[...].reshape(count * SPAN, LANES) * scale
    low_buf[...] = dot(long(b), back_buf[...]).reshape(count, SPAN, 4 * LANES)

    def out(k):
        return pltpu.make_async_copy(out_buf.at[k], out_ref.at[:, quantum(k), :], sems.at[k])

    def body(k, _):
        turned = lax.rem(k + count - lax.div(place[4], 2), count)
        out_buf[k] = back(bands_of(low_buf[turned]), low_rows[...])
        out(k).start()
        return 0

    lax.fori_loop(0, count, body, 0)
    for k in range(count):
        out(k).wait()


ANY = pl.BlockSpec(memory_space=pl.ANY)
BANDS = jax.ShapeDtypeStruct((PLANE, QUARTER, LANES), jnp.float32)


def call(kernel, place, operands, outs, scratch, aliases, vmem):
    scalars = [] if place is None else [place]
    return pl.pallas_call(
        kernel,
        grid_spec=pltpu.PrefetchScalarGridSpec(
            num_scalar_prefetch=len(scalars),
            grid=(),
            in_specs=[ANY] * len(operands),
            out_specs=[ANY] * len(outs),
            scratch_shapes=scratch,
        ),
        out_shape=outs,
        input_output_aliases=aliases,
        cost_estimate=pl.CostEstimate(flops=0, bytes_accessed=0, transcendentals=0),
        compiler_params=pltpu.CompilerParams(vmem_limit_bytes=vmem * 1024 * 1024),
    )(*scalars, *operands)


def floats(*shape):
    return jax.ShapeDtypeStruct(shape, jnp.float32)


def held(count, *dtypes):
    return [pltpu.VMEM((count, SPAN, QUANTUM, LANES), dtype) for dtype in dtypes]


def lows(count):
    return [pltpu.VMEM((count, SPAN, 4 * LANES), jnp.float32)]


def same(arrays):
    return [pltpu.VMEM(a.shape, a.dtype) for a in arrays]


def sems(*shape):
    return pltpu.SemaphoreType.DMA(shape)


def cast(place, g, *wanted):
    n = sum(count for _, _, count in wanted)
    return call(
        functools.partial(cast_kernel, wanted),
        place,
        [g],
        [floats(SPAN, count * QUANTUM, LANES) for _, _, count in wanted],
        held(n, jnp.bfloat16, jnp.float32) + [sems(2, n)],
        {},
        MOST,
    )


def encoded(place, g, received, first, counts, slot, mats, bands=None):
    values = [mats["rows"], mats["lanes"]]
    extra = int(bands is not None)
    sent = sum(counts)
    n = sent + extra
    return call(
        functools.partial(encode_kernel, first, counts, extra, slot, [r.shape[1] // QUANTUM for r in received]),
        place,
        [g, *received, *values, *([bands] * extra)],
        [floats(c, PAYLOAD, LANES) for c in counts] + [BANDS],
        held(n, jnp.bfloat16, jnp.float32)
        + [pltpu.VMEM((sent, PAYLOAD, LANES), jnp.float32), pltpu.VMEM((n, 2, QUARTER, LANES), jnp.float32)]
        + lows(n)
        + [pltpu.VMEM((2, QUARTER, LANES), jnp.float32)]
        + same(values)
        + [sems(5, n), sems(3)],
        {4 + len(received): len(counts)} if extra else {},
        MOST,
    )


def moments(place, m, g, early, received, slot, mats):
    values = [mats["low"], mats["band"]]
    counts = [r.shape[1] // QUANTUM for r in received]
    n = sum(counts)
    return call(
        functools.partial(moment_kernel, counts, slot),
        place,
        [m, g, early, *received, *values],
        [floats(*m.shape), BANDS],
        held(n, jnp.float32, jnp.bfloat16, jnp.float32)
        + [pltpu.VMEM((n, 2, QUARTER, LANES), jnp.float32)]
        + lows(n)
        + [pltpu.VMEM((SPAN, QUANTUM, LANES), jnp.float32)]
        + same(values)
        + [sems(5, n), sems(3)],
        {},
        MOST,
    )


def rest(place, cells, bands, g, received, slot, mats):
    values = [mats[name] for name in ("low", "low_back", "band", "band_back")]
    n = cells.shape[1] // QUANTUM
    one = [pltpu.VMEM((SPAN, QUANTUM, LANES), dtype) for dtype in (jnp.bfloat16, jnp.float32, jnp.float32)]
    return call(
        functools.partial(rest_kernel, slot),
        place,
        [cells, bands, g, received, *values],
        [
            floats(*cells.shape),
            floats(SPAN, QUANTUM, LANES),
            floats(SPLIT, QUANTUM, LANES),
            floats(SPAN - SPLIT, QUANTUM, LANES),
        ],
        held(n, jnp.float32)
        + [pltpu.VMEM(BANDS.shape, jnp.float32)]
        + lows(n + 1)
        + one
        + same(values)
        + [sems(2, n), sems(10)],
        {1: 0},
        MOST,
    )


def added(there, last, base, first, row):
    return call(
        functools.partial(add_kernel, first, row),
        None,
        [there, last, base],
        [floats(*base.shape)],
        same([there, there]) + [sems(3)],
        {2: 0},
        MOST,
    )[0]


def decoded(payload, base, first, mats):
    values = [mats["rows_back"], mats["kept_back"]]
    count = payload.shape[0]
    return call(
        functools.partial(decode_kernel, first, count),
        None,
        [payload, *values, base],
        [floats(*base.shape)],
        [pltpu.VMEM((count, PAYLOAD, LANES), jnp.float32)]
        + held(count, jnp.float32)
        + lows(count)
        + same(values)
        + [sems(3, count), sems(2)],
        {3: 0},
        MOST,
    )[0]


def updated(place, band, scale, shape, mats):
    values = [mats["low_back"], mats["band_back"]]
    count = shape[1] // QUANTUM
    return call(
        functools.partial(update_kernel, scale, count),
        place,
        [band, *values],
        [floats(*shape)],
        same([band, *values]) + held(count, jnp.float32) + lows(count) + [sems(count), sems(3)],
        {},
        MOST,
    )[0]


def tiles(x):
    rows, mats, width = x.shape
    x = x.reshape(rows, mats, width // LANES, LANES).transpose(0, 2, 1, 3)
    return x.reshape(rows, mats * width // LANES, LANES)


def untiles(x, mats):
    rows, places, _ = x.shape
    x = x.reshape(rows, places // mats, mats, LANES).transpose(0, 2, 1, 3)
    return x.reshape(rows, mats, places // mats * LANES)


def tie(*arrays):
    return lax.optimization_barrier(arrays)


def per_device(grads, momentum):
    rep_count = lax.axis_size("rep")
    mat_count = grads.shape[3]
    mats = constants()
    g = tiles(grads[0, 0])
    m = tiles(momentum[0])
    count = m.shape[1] // QUANTUM
    member = lax.axis_index("fsdp")
    turn = lax.axis_index("rep") // PLANE * TURN
    place = jnp.stack([member, member ^ 1, member ^ 2, member ^ 3, turn, TURN - turn]).astype(jnp.int32)
    over_core = [(f, f ^ 1) for f in range(4)]
    over_z = [(f, f ^ 2) for f in range(4)]

    def core(x):
        return lax.ppermute(x, "fsdp", over_core)

    def link(x):
        return lax.ppermute(x, "fsdp", over_z)

    def head(slot):
        return lax.dynamic_slice(g, (place[slot] * SPAN, 0, 0), (SPAN, QUANTUM, LANES)).astype(jnp.float32)

    place1, cells = tie(place, head(3))
    (more,) = cast(place1, g, (3, 1, SECOND))
    got, more = tie(core(cells), more)
    cells = head(2) + got
    early = link(cells)
    pay, other_band = encoded(place, g, [core(more)], 1, (SECOND,), 2, mats)
    second = link(pay)
    place2, _ = tie(place1, pay)
    wanted = [(3, k, 1) for k in range(1 + SECOND, count)] + [(1, k, 2) for k in range(0, count, 2)]
    *cells, later = cast(place2, g, *wanted)
    early, later, _ = tie(early, later, pay)
    pieces = [core(c) for c in [*cells, later]]
    got, mine = pieces[: -count // 2], pieces[-count // 2 :]
    pay, other_band = encoded(place, g, got, 1 + SECOND, (count - 2 - SECOND,), 2, mats, other_band)
    third = link(pay)
    names = ("rep", "fsdp")
    wrapped = lax.ppermute(other_band, names, steps(rep_count, 0, 2))
    cells, own_band = moments(place, m, g, early, mine, 0, mats)
    base, last, top, bottom = rest(place, cells, own_band, g, got[-1], 2, mats)

    groups = [[h * PLANE + i for i in range(PLANE)] for h in range(rep_count // PLANE)]
    met = lax.all_to_all(own_band + wrapped, "rep", 0, 0, axis_index_groups=groups, tiled=True)
    met, bottom = tie(met, bottom)
    top, bottom = link(top), link(bottom)
    part = jnp.sum(met.reshape(PLANE, QUARTER, LANES), axis=0)
    total = part + lax.ppermute(part, names, steps(rep_count, TURN, 0))
    total, second = tie(total, second)
    spread = jnp.broadcast_to(total[None], (PLANE,) + total.shape)
    band_total = lax.all_to_all(spread, "rep", 0, 0, axis_index_groups=groups, tiled=True)
    out, band_total = tie(decoded(second, base, 1, mats), band_total)
    update = updated(place, band_total, 1.0 / rep_count, m.shape, mats)

    third, update = tie(third, update)
    out = decoded(third, out, 1 + SECOND, mats)
    top, out = tie(top, out)
    out = added(top, last, out, count - 1, 0)
    bottom, out = tie(bottom, out)
    out = added(bottom, last, out, count - 1, SPLIT)
    return (untiles(out, mat_count)[None], untiles(update, mat_count))


def steps(rep_count, turn, member):
    pairs = []
    for rep in range(rep_count):
        high, low = divmod(rep, PLANE)
        to = (high ^ 1) * PLANE + (low + (turn if high else PLANE - turn)) % PLANE
        pairs += [(rep * 4 + f, to * 4 + (f ^ member)) for f in range(4)]
    return pairs


def solution(mesh):
    in_specs = (P("rep", "fsdp", None, None, None), P("rep", "fsdp", None, None))
    out_specs = (P("rep", "fsdp", None, None), P("fsdp", None, None))
    return jax.shard_map(
        per_device, mesh=mesh, in_specs=in_specs, out_specs=out_specs, check_vma=False
    )
```

```python
import functools
import math

import jax
import jax.numpy as jnp
import ml_dtypes
import numpy as np
from jax import lax
from jax.experimental import pallas as pl
from jax.experimental.pallas import tpu as pltpu
from jax.sharding import PartitionSpec as P

SPAN = 64
BAND = 16
LANES = 128
GROUP = 8
QUANTUM = 2 * GROUP
DECAY = 0.9
HIGH = SPAN - BAND
QUARTER = GROUP // 4 * BAND
PAYLOAD = QUANTUM * HIGH + 3 * SPAN
SECOND = 4
SPLIT = 48
PLANE = 16
TURN = 4
MOST = 46


def dct(order):
    q = np.arange(order)[:, None]
    n = np.arange(order)[None, :]
    scale = np.where(q == 0, math.sqrt(1.0 / order), math.sqrt(2.0 / order))
    return scale * np.cos(math.pi * (2 * n + 1) * q / (2 * order))


def halves(a):
    high = a.astype(ml_dtypes.bfloat16)
    return high, (a - high.astype(np.float64)).astype(ml_dtypes.bfloat16)


def left(a):
    high, low = halves(a)
    return np.concatenate([high, low, high], axis=1)


def right(a):
    high, low = halves(a)
    return np.concatenate([high, low, high], axis=0)


def constants():
    t = dct(SPAN)
    lanes = np.kron(np.eye(8), t.T)
    coef = np.arange(512) % SPAN
    order = np.concatenate([np.flatnonzero(coef >= BAND), np.flatnonzero(coef < BAND)])
    lanes = lanes[:, order]
    kept, band = lanes[:, : 3 * LANES], lanes[:, 3 * LANES :]
    mats = dict(
        rows=left(t), rows_back=left(t.T), low=left(t[:BAND]), low_back=left(t[:BAND].T),
        lanes=right(lanes), kept_back=right(kept.T), band=right(band), band_back=right(band.T),
    )
    return {name: jnp.asarray(a) for name, a in mats.items()}


def split(x):
    high = x.astype(jnp.bfloat16)
    return high, (x - high.astype(jnp.float32)).astype(jnp.bfloat16)


def tall(x):
    high, low = split(x)
    return jnp.concatenate([high, high, low], axis=0)


def long(x):
    high, low = split(x)
    return jnp.concatenate([high, high, low], axis=1)


def dot(a, b):
    return jnp.dot(a, b, preferred_element_type=jnp.float32)


def beside(x):
    x = jnp.swapaxes(x, 0, 1)
    return [jnp.concatenate([x[4 * s + j] for j in range(4)], axis=1) for s in range(4)]


def apart(parts):
    x = jnp.stack([p[:, j * LANES : (j + 1) * LANES] for p in parts for j in range(4)], axis=0)
    return jnp.swapaxes(x, 0, 1)


def forward(x, rows):
    return [dot(rows, tall(part)) for part in beside(x)]


def back(parts, rows):
    return apart([dot(rows, tall(p)) for p in parts])


def bands_of(c):
    return [c[s * BAND : (s + 1) * BAND] for s in range(4)]


def rows_of(slot):
    member = lax.axis_index("fsdp") ^ slot
    return pl.ds(pl.multiple_of(member * SPAN, SPAN), SPAN)


def turn(other=False):
    own = lax.div(lax.axis_index("rep"), PLANE) * TURN
    return TURN - own if other else own


def quantum(k):
    return pl.ds(k * QUANTUM, QUANTUM)


def band_at(k, shift):
    return pl.ds(lax.rem(2 * k + PLANE - shift, PLANE), 2)


def load(constants, buffers, sems):
    copies = [pltpu.make_async_copy(c, b, sems.at[i]) for i, (c, b) in enumerate(zip(constants, buffers))]
    for copy in copies:
        copy.start()
    return copies


def cast_kernel(wanted, place, g_ref, *refs):
    outs, (held, cells, sems) = refs[: len(wanted)], refs[len(wanted) :]
    into, out = [], []
    for o, (slot, first, n) in zip(outs, wanted):
        for j in range(n):
            k = len(into)
            source = g_ref.at[rows_of(slot), quantum(first + j), :]
            into.append(pltpu.make_async_copy(source, held.at[k], sems.at[0, k]))
            out.append(pltpu.make_async_copy(cells.at[k], o.at[:, quantum(j), :], sems.at[1, k]))
            into[-1].start()
    for k in range(len(into)):
        into[k].wait()
        cells[k] = held[k].astype(jnp.float32)
        out[k].start()
    for copy in out:
        copy.wait()


def encode_kernel(first, counts, extra, slot, received, place, g_ref, *refs):
    come = [(ref, j) for ref, n in zip(refs, received) for j in range(n)]
    rows, lanes, *refs = refs[len(received) :]
    refs = refs[extra:]
    pays, refs = refs[: len(counts)], refs[len(counts) :]
    band_ref, g_buf, r_buf, pay_buf, band_buf, low_buf, zero_buf, rows_buf, lanes_buf, sems, more_sems = refs
    high = QUANTUM * HIGH
    sent = sum(counts)
    count = sent + extra
    where = [(ref, j) for ref, n in zip(pays, counts) for j in range(n)]
    other_turn = turn(other=True)

    def into(k, ref=None, j=0):
        ref = come[0][0] if ref is None else ref
        yield pltpu.make_async_copy(g_ref.at[rows_of(slot), quantum(first + k), :], g_buf.at[k], sems.at[0, k])
        yield pltpu.make_async_copy(ref.at[:, quantum(j), :], r_buf.at[k], sems.at[1, k])

    def out_high(k, ref, j):
        at = pl.ds(0, high)
        return pltpu.make_async_copy(pay_buf.at[k, at], ref.at[j, at], sems.at[2, k])

    def out_low(k, ref, j):
        at = pl.ds(high, 3 * SPAN)
        return pltpu.make_async_copy(pay_buf.at[k, at], ref.at[j, at], sems.at[3, k])

    def out_band(k):
        return pltpu.make_async_copy(band_buf.at[k], band_ref.at[band_at(first + k, other_turn)], sems.at[4, k])

    if not extra:
        blank = pltpu.make_async_copy(zero_buf, band_ref.at[band_at(0, other_turn)], more_sems.at[2])
    for copy in into(0, *come[0]):
        copy.start()
    consts = load((rows, lanes), (rows_buf, lanes_buf), more_sems)
    for k in range(1, count):
        for copy in into(k, *come[k]):
            copy.start()
    if not extra:
        zero_buf[...] = jnp.zeros_like(zero_buf)
        blank.start()
    consts[0].wait()

    def low_of(k, c, s):
        low_buf[k, s * BAND : (s + 1) * BAND, :] = c[:BAND]

    def cells_of(k):
        for copy in into(k):
            copy.wait()
        return g_buf[k].astype(jnp.float32) + r_buf[k]

    def body(k, _):
        for s, c in enumerate(forward(cells_of(k), rows_buf[...])):
            low_of(k, c, s)
            for j in range(4):
                at = (4 * s + j) * HIGH
                pay_buf[k, at : at + HIGH, :] = c[BAND:, j * LANES : (j + 1) * LANES]
        for i, ref in enumerate(pays):
            start = sum(counts[:i])

            @pl.when((k >= start) & (k < start + counts[i]))
            def _():
                out_high(k, ref, k - start).start()

        return 0

    lax.fori_loop(0, sent, body, 0)
    for k in range(sent, count):
        for s, c in enumerate(forward(cells_of(k), rows_buf[:BAND, :])):
            low_of(k, c, s)
    consts[1].wait()
    w = dot(long(low_buf[...].reshape(count * SPAN, 4 * LANES)), lanes_buf[...])
    for k in range(count):
        part = w[k * SPAN : (k + 1) * SPAN]
        if k < sent:
            for i in range(3):
                at = high + i * SPAN
                pay_buf[k, at : at + SPAN, :] = part[:, i * LANES : (i + 1) * LANES]
            out_low(k, *where[k]).start()
        band_buf[k] = part[:, 3 * LANES :].reshape(2, QUARTER, LANES)
        out_band(k).start()
    for k in range(count):
        if k < sent:
            out_high(k, *where[k]).wait()
            out_low(k, *where[k]).wait()
        out_band(k).wait()
    if not extra:
        blank.wait()


def moment_kernel(counts, slot, place, m_ref, g_ref, early_ref, *refs):
    received, refs = refs[: len(counts)], refs[len(counts) :]
    constants, refs = refs[:2], refs[2:]
    cells_ref, band_ref, m_buf, g_buf, r_buf, band_buf, low_buf, early_buf = refs[:8]
    buffers, (sems, more_sems) = refs[8:10], refs[10:]
    own_turn = turn()
    total = sum(counts)
    where = [(r, j) for r, n in zip(received, counts) for j in range(n)]

    def into(k, r=None, j=0):
        r = received[0] if r is None else r
        yield pltpu.make_async_copy(g_ref.at[rows_of(slot), quantum(k), :], g_buf.at[k], sems.at[0, k])
        yield pltpu.make_async_copy(r.at[:, quantum(j), :], r_buf.at[k], sems.at[1, k])
        yield pltpu.make_async_copy(m_ref.at[:, quantum(k), :], m_buf.at[k], sems.at[2, k])

    def out(k):
        return pltpu.make_async_copy(m_buf.at[k], cells_ref.at[:, quantum(k), :], sems.at[3, k])

    def out_band(k):
        return pltpu.make_async_copy(band_buf.at[k], band_ref.at[band_at(k, own_turn)], sems.at[4, k])

    early = pltpu.make_async_copy(early_ref, early_buf, more_sems.at[2])
    for copy in (*into(0, *where[0]), early):
        copy.start()
    consts = load(constants, buffers, more_sems)
    for k in range(1, total):
        for copy in into(k, *where[k]):
            copy.start()
    for copy in consts:
        copy.wait()
    low, band = buffers

    def cells_of(k, more=None):
        for copy in into(k):
            copy.wait()
        cells = DECAY * m_buf[k] + (g_buf[k].astype(jnp.float32) + r_buf[k])
        if more is not None:
            cells = cells + more
        m_buf[k] = cells
        out(k).start()
        for s, c in enumerate(forward(cells, low[...])):
            low_buf[k, s * BAND : (s + 1) * BAND, :] = c

    def body(k, _):
        cells_of(k)
        return 0

    early.wait()
    cells_of(0, early_buf[...])
    lax.fori_loop(1, total, body, 0)
    b = dot(long(low_buf[...].reshape(total * SPAN, 4 * LANES)), band[...])
    band_buf[...] = b.reshape(total, 2, QUARTER, LANES)
    for k in range(total):
        out_band(k).start()
    for k in range(total):
        out(k).wait()
        out_band(k).wait()


def rest_kernel(slot, place, cells_ref, bands_ref, g_ref, r_ref, *refs):
    constants, refs = refs[:4], refs[4:]
    out_ref, last_ref, top_ref, bottom_ref = refs[:4]
    cells_buf, band_buf, low_buf, g_buf, r_buf, theirs_buf = refs[4:10]
    buffers, (sems, more_sems) = refs[10:14], refs[14:]
    own_turn = turn()
    total = cells_buf.shape[0]
    split = top_ref.shape[0]

    def into(k):
        return pltpu.make_async_copy(cells_ref.at[:, quantum(k), :], cells_buf.at[k], sems.at[0, k])

    def out(k):
        return pltpu.make_async_copy(cells_buf.at[k], out_ref.at[:, quantum(k), :], sems.at[1, k])

    def out_last():
        yield pltpu.make_async_copy(cells_buf.at[total - 1], last_ref, more_sems.at[4])
        yield pltpu.make_async_copy(theirs_buf.at[pl.ds(0, split)], top_ref, more_sems.at[5])
        yield pltpu.make_async_copy(theirs_buf.at[pl.ds(split, SPAN - split)], bottom_ref, more_sems.at[6])

    theirs = [
        pltpu.make_async_copy(g_ref.at[rows_of(slot), quantum(total - 1), :], g_buf, more_sems.at[7]),
        pltpu.make_async_copy(r_ref.at[:, quantum(r_ref.shape[1] // QUANTUM - 1), :], r_buf, more_sems.at[8]),
        pltpu.make_async_copy(bands_ref, band_buf, more_sems.at[9]),
    ]
    for copy in theirs:
        copy.start()
    consts = load(constants, buffers, more_sems)
    for k in range(total):
        into(k).start()
    for copy in (*theirs, *consts):
        copy.wait()
    low, low_back, band, band_back = buffers

    theirs_buf[...] = g_buf[...].astype(jnp.float32) + r_buf[...]
    c = jnp.concatenate(forward(theirs_buf[...], low[...]), axis=0)
    theirs_band = dot(long(c), band[...])
    b = jnp.concatenate([band_buf[...].reshape(total * SPAN, LANES), theirs_band], axis=0)
    low_buf[...] = dot(long(b), band_back[...]).reshape(total + 1, SPAN, 4 * LANES)
    theirs_buf[...] = theirs_buf[...] - back(bands_of(low_buf[total]), low_back[...])

    def body(k, _):
        into(k).wait()
        turned = lax.rem(k + total - lax.div(own_turn, 2), total)
        cells_buf[k] = cells_buf[k] - back(bands_of(low_buf[turned]), low_back[...])

        @pl.when(k < total - 1)
        def _():
            out(k).start()

        return 0

    lax.fori_loop(0, total, body, 0)
    for copy in out_last():
        copy.start()
    for k in range(total - 1):
        out(k).wait()
    for copy in out_last():
        copy.wait()


def decode_kernel(first, count, pay_ref, rows_back, kept_back, base_ref, out_ref, *refs):
    pay_buf, base_buf, low_buf, rows_buf, kept_buf, sems, const_sems = refs
    at = QUANTUM * HIGH

    def into(k):
        yield pltpu.make_async_copy(pay_ref.at[k], pay_buf.at[k], sems.at[0, k])
        yield pltpu.make_async_copy(base_ref.at[:, quantum(first + k), :], base_buf.at[k], sems.at[1, k])

    def out(k):
        return pltpu.make_async_copy(base_buf.at[k], out_ref.at[:, quantum(first + k), :], sems.at[2, k])

    for k in range(count):
        for copy in into(k):
            copy.start()
    for copy in load((rows_back, kept_back), (rows_buf, kept_buf), const_sems):
        copy.wait()
    for k in range(count):
        for copy in into(k):
            copy.wait()
    kept = [
        jnp.concatenate([pay_buf[k, at + i * SPAN : at + (i + 1) * SPAN, :] for i in range(3)], axis=1)
        for k in range(count)
    ]
    low_buf[...] = dot(long(jnp.concatenate(kept, axis=0)), kept_buf[...]).reshape(count, SPAN, 4 * LANES)

    def body(k, _):
        parts = []
        for s, low in enumerate(bands_of(low_buf[k])):
            high = [pay_buf[k, (4 * s + j) * HIGH : (4 * s + j + 1) * HIGH, :] for j in range(4)]
            parts.append(jnp.concatenate([low, jnp.concatenate(high, axis=1)], axis=0))
        base_buf[k] = base_buf[k] + back(parts, rows_buf[...])
        out(k).start()
        return 0

    lax.fori_loop(0, count, body, 0)
    for k in range(count):
        out(k).wait()


def add_kernel(first, row, there_ref, last_ref, base_ref, out_ref, there_buf, last_buf, sems):
    rows = pl.ds(row, there_ref.shape[0])
    into = [
        pltpu.make_async_copy(there_ref, there_buf, sems.at[0]),
        pltpu.make_async_copy(last_ref.at[rows], last_buf, sems.at[1]),
    ]
    for copy in into:
        copy.start()
    for copy in into:
        copy.wait()
    last_buf[...] += there_buf[...]
    out = pltpu.make_async_copy(last_buf, out_ref.at[rows, quantum(first)], sems.at[2])
    out.start()
    out.wait()


def update_kernel(scale, count, place, band_ref, low_back, band_back, out_ref, band_buf, low_rows, back_buf, out_buf, low_buf, sems, const_sems):
    own_turn = turn()
    for copy in load((band_ref, low_back, band_back), (band_buf, low_rows, back_buf), const_sems):
        copy.wait()
    b = band_buf[...].reshape(count * SPAN, LANES) * scale
    low_buf[...] = dot(long(b), back_buf[...]).reshape(count, SPAN, 4 * LANES)

    def out(k):
        return pltpu.make_async_copy(out_buf.at[k], out_ref.at[:, quantum(k), :], sems.at[k])

    def body(k, _):
        turned = lax.rem(k + count - lax.div(own_turn, 2), count)
        out_buf[k] = back(bands_of(low_buf[turned]), low_rows[...])
        out(k).start()
        return 0

    lax.fori_loop(0, count, body, 0)
    for k in range(count):
        out(k).wait()


ANY = pl.BlockSpec(memory_space=pl.ANY)
BANDS = jax.ShapeDtypeStruct((PLANE, QUARTER, LANES), jnp.float32)


def call(kernel, place, operands, outs, scratch, aliases, vmem):
    operands = operands if place is None else [place, *operands]
    return pl.pallas_call(
        kernel,
        grid_spec=pltpu.PrefetchScalarGridSpec(
            num_scalar_prefetch=0,
            grid=(),
            in_specs=[ANY] * len(operands),
            out_specs=[ANY] * len(outs),
            scratch_shapes=scratch,
        ),
        out_shape=outs,
        input_output_aliases=aliases,
        cost_estimate=pl.CostEstimate(flops=0, bytes_accessed=0, transcendentals=0),
        compiler_params=pltpu.CompilerParams(vmem_limit_bytes=vmem * 1024 * 1024),
    )(*operands)


def floats(*shape):
    return jax.ShapeDtypeStruct(shape, jnp.float32)


def held(count, *dtypes):
    return [pltpu.VMEM((count, SPAN, QUANTUM, LANES), dtype) for dtype in dtypes]


def lows(count):
    return [pltpu.VMEM((count, SPAN, 4 * LANES), jnp.float32)]


def same(arrays):
    return [pltpu.VMEM(a.shape, a.dtype) for a in arrays]


def sems(*shape):
    return pltpu.SemaphoreType.DMA(shape)


def cast(place, g, *wanted):
    n = sum(count for _, _, count in wanted)
    return call(
        functools.partial(cast_kernel, wanted),
        place,
        [g],
        [floats(SPAN, count * QUANTUM, LANES) for _, _, count in wanted],
        held(n, jnp.bfloat16, jnp.float32) + [sems(2, n)],
        {},
        MOST,
    )


def encoded(place, g, received, first, counts, slot, mats, bands=None):
    values = [mats["rows"], mats["lanes"]]
    extra = int(bands is not None)
    sent = sum(counts)
    n = sent + extra
    return call(
        functools.partial(encode_kernel, first, counts, extra, slot, [r.shape[1] // QUANTUM for r in received]),
        place,
        [g, *received, *values, *([bands] * extra)],
        [floats(c, PAYLOAD, LANES) for c in counts] + [BANDS],
        held(n, jnp.bfloat16, jnp.float32)
        + [pltpu.VMEM((sent, PAYLOAD, LANES), jnp.float32), pltpu.VMEM((n, 2, QUARTER, LANES), jnp.float32)]
        + lows(n)
        + [pltpu.VMEM((2, QUARTER, LANES), jnp.float32)]
        + same(values)
        + [sems(5, n), sems(3)],
        {4 + len(received): len(counts)} if extra else {},
        MOST,
    )


def moments(place, m, g, early, received, slot, mats):
    values = [mats["low"], mats["band"]]
    counts = [r.shape[1] // QUANTUM for r in received]
    n = sum(counts)
    return call(
        functools.partial(moment_kernel, counts, slot),
        place,
        [m, g, early, *received, *values],
        [floats(*m.shape), BANDS],
        held(n, jnp.float32, jnp.bfloat16, jnp.float32)
        + [pltpu.VMEM((n, 2, QUARTER, LANES), jnp.float32)]
        + lows(n)
        + [pltpu.VMEM((SPAN, QUANTUM, LANES), jnp.float32)]
        + same(values)
        + [sems(5, n), sems(3)],
        {},
        MOST,
    )


def rest(place, cells, bands, g, received, slot, mats):
    values = [mats[name] for name in ("low", "low_back", "band", "band_back")]
    n = cells.shape[1] // QUANTUM
    one = [pltpu.VMEM((SPAN, QUANTUM, LANES), dtype) for dtype in (jnp.bfloat16, jnp.float32, jnp.float32)]
    return call(
        functools.partial(rest_kernel, slot),
        place,
        [cells, bands, g, received, *values],
        [
            floats(*cells.shape),
            floats(SPAN, QUANTUM, LANES),
            floats(SPLIT, QUANTUM, LANES),
            floats(SPAN - SPLIT, QUANTUM, LANES),
        ],
        held(n, jnp.float32)
        + [pltpu.VMEM(BANDS.shape, jnp.float32)]
        + lows(n + 1)
        + one
        + same(values)
        + [sems(2, n), sems(10)],
        {1: 0},
        MOST,
    )


def added(there, last, base, first, row):
    return call(
        functools.partial(add_kernel, first, row),
        None,
        [there, last, base],
        [floats(*base.shape)],
        same([there, there]) + [sems(3)],
        {2: 0},
        MOST,
    )[0]


def decoded(payload, base, first, mats):
    values = [mats["rows_back"], mats["kept_back"]]
    count = payload.shape[0]
    return call(
        functools.partial(decode_kernel, first, count),
        None,
        [payload, *values, base],
        [floats(*base.shape)],
        [pltpu.VMEM((count, PAYLOAD, LANES), jnp.float32)]
        + held(count, jnp.float32)
        + lows(count)
        + same(values)
        + [sems(3, count), sems(2)],
        {3: 0},
        MOST,
    )[0]


def updated(place, band, scale, shape, mats):
    values = [mats["low_back"], mats["band_back"]]
    count = shape[1] // QUANTUM
    return call(
        functools.partial(update_kernel, scale, count),
        place,
        [band, *values],
        [floats(*shape)],
        same([band, *values]) + held(count, jnp.float32) + lows(count) + [sems(count), sems(3)],
        {},
        MOST,
    )[0]


def tiles(x):
    rows, mats, width = x.shape
    x = x.reshape(rows, mats, width // LANES, LANES).transpose(0, 2, 1, 3)
    return x.reshape(rows, mats * width // LANES, LANES)


def untiles(x, mats):
    rows, places, _ = x.shape
    x = x.reshape(rows, places // mats, mats, LANES).transpose(0, 2, 1, 3)
    return x.reshape(rows, mats, places // mats * LANES)


def tie(*arrays):
    return lax.optimization_barrier(arrays)


def per_device(grads, momentum):
    rep_count = lax.axis_size("rep")
    mat_count = grads.shape[3]
    mats = constants()
    g = tiles(grads[0, 0])
    m = tiles(momentum[0])
    count = m.shape[1] // QUANTUM
    member = lax.axis_index("fsdp")
    place = jnp.full((8, LANES), member, jnp.int32)
    over_core = [(f, f ^ 1) for f in range(4)]
    over_z = [(f, f ^ 2) for f in range(4)]

    def core(x):
        return lax.ppermute(x, "fsdp", over_core)

    def link(x):
        return lax.ppermute(x, "fsdp", over_z)

    def head(slot):
        return lax.dynamic_slice(g, ((member ^ slot) * SPAN, 0, 0), (SPAN, QUANTUM, LANES)).astype(jnp.float32)

    place1, cells = tie(place, head(3))
    more, own = cast(place1, g, (3, 1, SECOND), (2, 0, 1))
    got, more = tie(core(cells), more)
    cells = own + got
    early = link(cells)
    pay, other_band = encoded(place, g, [core(more)], 1, (SECOND,), 2, mats)
    second = link(pay)
    place2, _ = tie(place1, pay)
    wanted = [(3, k, 1) for k in range(1 + SECOND, count)] + [(1, k, 2) for k in range(0, count, 2)]
    *cells, later = cast(place2, g, *wanted)
    early, later, _ = tie(early, later, pay)
    pieces = [core(c) for c in [*cells, later]]
    got, mine = pieces[: -count // 2], pieces[-count // 2 :]
    pay, other_band = encoded(place, g, got, 1 + SECOND, (count - 2 - SECOND,), 2, mats, other_band)
    third = link(pay)
    names = ("rep", "fsdp")
    wrapped = lax.ppermute(other_band, names, steps(rep_count, 0, 2))
    cells, own_band = moments(place, m, g, early, mine, 0, mats)
    base, last, top, bottom = rest(place, cells, own_band, g, got[-1], 2, mats)

    groups = [[h * PLANE + i for i in range(PLANE)] for h in range(rep_count // PLANE)]
    met = lax.all_to_all(own_band + wrapped, "rep", 0, 0, axis_index_groups=groups, tiled=True)
    met, bottom = tie(met, bottom)
    top, bottom = link(top), link(bottom)
    part = jnp.sum(met.reshape(PLANE, QUARTER, LANES), axis=0)
    total = part + lax.ppermute(part, names, steps(rep_count, TURN, 0))
    total, second = tie(total, second)
    spread = jnp.broadcast_to(total[None], (PLANE,) + total.shape)
    band_total = lax.all_to_all(spread, "rep", 0, 0, axis_index_groups=groups, tiled=True)
    out, band_total = tie(decoded(second, base, 1, mats), band_total)
    update = updated(place, band_total, 1.0 / rep_count, m.shape, mats)

    third, update = tie(third, update)
    out = decoded(third, out, 1 + SECOND, mats)
    top, out = tie(top, out)
    out = added(top, last, out, count - 1, 0)
    bottom, out = tie(bottom, out)
    out = added(bottom, last, out, count - 1, SPLIT)
    return (untiles(out, mat_count)[None], untiles(update, mat_count))


def steps(rep_count, turn, member):
    pairs = []
    for rep in range(rep_count):
        high, low = divmod(rep, PLANE)
        to = (high ^ 1) * PLANE + (low + (turn if high else PLANE - turn)) % PLANE
        pairs += [(rep * 4 + f, to * 4 + (f ^ member)) for f in range(4)]
    return pairs


def solution(mesh):
    in_specs = (P("rep", "fsdp", None, None, None), P("rep", "fsdp", None, None))
    out_specs = (P("rep", "fsdp", None, None), P("fsdp", None, None))
    return jax.shard_map(
        per_device, mesh=mesh, in_specs=in_specs, out_specs=out_specs, check_vma=False
    )
```

```python
import functools
import math

import jax
import jax.numpy as jnp
import ml_dtypes
import numpy as np
from jax import lax
from jax.experimental import pallas as pl
from jax.experimental.pallas import tpu as pltpu
from jax.sharding import PartitionSpec as P

SPAN = 64
BAND = 16
LANES = 128
GROUP = 8
QUANTUM = 2 * GROUP
DECAY = 0.9
HIGH = SPAN - BAND
QUARTER = GROUP // 4 * BAND
PAYLOAD = QUANTUM * HIGH + 3 * SPAN
SECOND = 4
SPLIT = 48
PLANE = 16
TURN = 4
MOST = 46


def dct(order):
    q = np.arange(order)[:, None]
    n = np.arange(order)[None, :]
    scale = np.where(q == 0, math.sqrt(1.0 / order), math.sqrt(2.0 / order))
    return scale * np.cos(math.pi * (2 * n + 1) * q / (2 * order))


def halves(a):
    high = a.astype(ml_dtypes.bfloat16)
    return high, (a - high.astype(np.float64)).astype(ml_dtypes.bfloat16)


def left(a):
    high, low = halves(a)
    return np.concatenate([high, low, high], axis=1)


def right(a):
    high, low = halves(a)
    return np.concatenate([high, low, high], axis=0)


def constants():
    t = dct(SPAN)
    lanes = np.kron(np.eye(8), t.T)
    coef = np.arange(512) % SPAN
    order = np.concatenate([np.flatnonzero(coef >= BAND), np.flatnonzero(coef < BAND)])
    lanes = lanes[:, order]
    kept, band = lanes[:, : 3 * LANES], lanes[:, 3 * LANES :]
    mats = dict(
        rows=left(t), rows_back=left(t.T), low=left(t[:BAND]), low_back=left(t[:BAND].T),
        lanes=right(lanes), kept=right(kept), kept_back=right(kept.T), band=right(band), band_back=right(band.T),
    )
    return {name: jnp.asarray(a) for name, a in mats.items()}


def split(x):
    high = x.astype(jnp.bfloat16)
    return high, (x - high.astype(jnp.float32)).astype(jnp.bfloat16)


def tall(x):
    high, low = split(x)
    return jnp.concatenate([high, high, low], axis=0)


def long(x):
    high, low = split(x)
    return jnp.concatenate([high, high, low], axis=1)


def dot(a, b):
    return jnp.dot(a, b, preferred_element_type=jnp.float32)


def beside(x):
    x = jnp.swapaxes(x, 0, 1)
    return [jnp.concatenate([x[4 * s + j] for j in range(4)], axis=1) for s in range(4)]


def apart(parts):
    x = jnp.stack([p[:, j * LANES : (j + 1) * LANES] for p in parts for j in range(4)], axis=0)
    return jnp.swapaxes(x, 0, 1)


def forward(x, rows):
    return [dot(rows, tall(part)) for part in beside(x)]


def back(parts, rows):
    return apart([dot(rows, tall(p)) for p in parts])


def bands_of(c):
    return [c[s * BAND : (s + 1) * BAND] for s in range(4)]


def rows_of(slot):
    member = lax.axis_index("fsdp") ^ slot
    return pl.ds(pl.multiple_of(member * SPAN, SPAN), SPAN)


def turn(other=False):
    own = lax.div(lax.axis_index("rep"), PLANE) * TURN
    return TURN - own if other else own


def quantum(k):
    return pl.ds(k * QUANTUM, QUANTUM)


def band_at(k, shift):
    return pl.ds(lax.rem(2 * k + PLANE - shift, PLANE), 2)


def load(constants, buffers, sems):
    copies = [pltpu.make_async_copy(c, b, sems.at[i]) for i, (c, b) in enumerate(zip(constants, buffers))]
    for copy in copies:
        copy.start()
    return copies


def cast_kernel(wanted, place, g_ref, *refs):
    outs, (held, cells, sems) = refs[: len(wanted)], refs[len(wanted) :]
    into, out = [], []
    for o, (slot, first, n) in zip(outs, wanted):
        for j in range(n):
            k = len(into)
            source = g_ref.at[rows_of(slot), quantum(first + j), :]
            into.append(pltpu.make_async_copy(source, held.at[k], sems.at[0, k]))
            out.append(pltpu.make_async_copy(cells.at[k], o.at[:, quantum(j), :], sems.at[1, k]))
            into[-1].start()
    for k in range(len(into)):
        into[k].wait()
        cells[k] = held[k].astype(jnp.float32)
        out[k].start()
    for copy in out:
        copy.wait()


def encode_kernel(first, counts, extra, slot, received, place, g_ref, *refs):
    come = [(ref, j) for ref, n in zip(refs, received) for j in range(n)]
    rows, lanes, *refs = refs[len(received) :]
    refs = refs[extra:]
    pays, refs = refs[: len(counts)], refs[len(counts) :]
    band_ref, g_buf, r_buf, pay_buf, band_buf, low_buf, zero_buf, rows_buf, lanes_buf, sems, more_sems = refs
    high = QUANTUM * HIGH
    sent = sum(counts)
    count = sent + extra
    where = [(ref, j) for ref, n in zip(pays, counts) for j in range(n)]
    other_turn = turn(other=True)

    def into(k, ref=None, j=0):
        ref = come[0][0] if ref is None else ref
        yield pltpu.make_async_copy(g_ref.at[rows_of(slot), quantum(first + k), :], g_buf.at[k], sems.at[0, k])
        yield pltpu.make_async_copy(ref.at[:, quantum(j), :], r_buf.at[k], sems.at[1, k])

    def out_high(k, ref, j):
        at = pl.ds(0, high)
        return pltpu.make_async_copy(pay_buf.at[k, at], ref.at[j, at], sems.at[2, k])

    def out_low(k, ref, j):
        at = pl.ds(high, 3 * SPAN)
        return pltpu.make_async_copy(pay_buf.at[k, at], ref.at[j, at], sems.at[3, k])

    def out_band(k):
        return pltpu.make_async_copy(band_buf.at[k], band_ref.at[band_at(first + k, other_turn)], sems.at[4, k])

    if not extra:
        blank = pltpu.make_async_copy(zero_buf, band_ref.at[band_at(0, other_turn)], more_sems.at[2])
    for copy in into(0, *come[0]):
        copy.start()
    consts = load((rows, lanes), (rows_buf, lanes_buf), more_sems)
    for k in range(1, count):
        for copy in into(k, *come[k]):
            copy.start()
    if not extra:
        zero_buf[...] = jnp.zeros_like(zero_buf)
        blank.start()
    consts[0].wait()

    def low_of(k, c, s):
        low_buf[k, s * BAND : (s + 1) * BAND, :] = c[:BAND]

    def cells_of(k):
        for copy in into(k):
            copy.wait()
        return g_buf[k].astype(jnp.float32) + r_buf[k]

    def body(k, _):
        for s, c in enumerate(forward(cells_of(k), rows_buf[...])):
            low_of(k, c, s)
            for j in range(4):
                at = (4 * s + j) * HIGH
                pay_buf[k, at : at + HIGH, :] = c[BAND:, j * LANES : (j + 1) * LANES]
        for i, ref in enumerate(pays):
            start = sum(counts[:i])

            @pl.when((k >= start) & (k < start + counts[i]))
            def _():
                out_high(k, ref, k - start).start()

        return 0

    lax.fori_loop(0, sent, body, 0)
    for k in range(sent, count):
        for s, c in enumerate(forward(cells_of(k), rows_buf[:BAND, :])):
            low_of(k, c, s)
    consts[1].wait()
    w = dot(long(low_buf[...].reshape(count * SPAN, 4 * LANES)), lanes_buf[...])
    for k in range(count):
        part = w[k * SPAN : (k + 1) * SPAN]
        if k < sent:
            for i in range(3):
                at = high + i * SPAN
                pay_buf[k, at : at + SPAN, :] = part[:, i * LANES : (i + 1) * LANES]
            out_low(k, *where[k]).start()
        band_buf[k] = part[:, 3 * LANES :].reshape(2, QUARTER, LANES)
        out_band(k).start()
    for k in range(count):
        if k < sent:
            out_high(k, *where[k]).wait()
            out_low(k, *where[k]).wait()
        out_band(k).wait()
    if not extra:
        blank.wait()


def moment_kernel(counts, slot, place, m_ref, g_ref, early_ref, *refs):
    received, refs = refs[: len(counts)], refs[len(counts) :]
    constants, refs = refs[:2], refs[2:]
    cells_ref, band_ref, m_buf, g_buf, r_buf, band_buf, low_buf, early_buf = refs[:8]
    buffers, (sems, more_sems) = refs[8:10], refs[10:]
    own_turn = turn()
    total = sum(counts)
    where = [(r, j) for r, n in zip(received, counts) for j in range(n)]

    def into(k, r=None, j=0):
        r = received[0] if r is None else r
        yield pltpu.make_async_copy(g_ref.at[rows_of(slot), quantum(k), :], g_buf.at[k], sems.at[0, k])
        yield pltpu.make_async_copy(r.at[:, quantum(j), :], r_buf.at[k], sems.at[1, k])
        yield pltpu.make_async_copy(m_ref.at[:, quantum(k), :], m_buf.at[k], sems.at[2, k])

    def out(k):
        return pltpu.make_async_copy(m_buf.at[k], cells_ref.at[:, quantum(k), :], sems.at[3, k])

    def out_band(k):
        return pltpu.make_async_copy(band_buf.at[k], band_ref.at[band_at(k, own_turn)], sems.at[4, k])

    early = pltpu.make_async_copy(early_ref, early_buf, more_sems.at[2])
    for copy in (*into(0, *where[0]), early):
        copy.start()
    consts = load(constants, buffers, more_sems)
    for k in range(1, total):
        for copy in into(k, *where[k]):
            copy.start()
    for copy in consts:
        copy.wait()
    low, band = buffers

    def cells_of(k, more=None):
        for copy in into(k):
            copy.wait()
        cells = DECAY * m_buf[k] + (g_buf[k].astype(jnp.float32) + r_buf[k])
        if more is not None:
            cells = cells + more
        m_buf[k] = cells
        out(k).start()
        for s, c in enumerate(forward(cells, low[...])):
            low_buf[k, s * BAND : (s + 1) * BAND, :] = c

    def body(k, _):
        cells_of(k)
        return 0

    early.wait()
    cells_of(0, early_buf[...])
    lax.fori_loop(1, total, body, 0)
    b = dot(long(low_buf[...].reshape(total * SPAN, 4 * LANES)), band[...])
    band_buf[...] = b.reshape(total, 2, QUARTER, LANES)
    for k in range(total):
        out_band(k).start()
    for k in range(total):
        out(k).wait()
        out_band(k).wait()


def rest_kernel(slot, place, cells_ref, bands_ref, g_ref, r_ref, *refs):
    constants, refs = refs[:5], refs[5:]
    out_ref, last_ref, half_ref, top_ref, bottom_ref = refs[:5]
    cells_buf, band_buf, low_buf, g_buf, r_buf, half_buf, raw_buf = refs[5:12]
    buffers, (sems, more_sems) = refs[12:17], refs[17:]
    own_turn = turn()
    total = cells_buf.shape[0]
    split = top_ref.shape[0]

    def into(k):
        return pltpu.make_async_copy(cells_ref.at[:, quantum(k), :], cells_buf.at[k], sems.at[0, k])

    def out(k):
        return pltpu.make_async_copy(cells_buf.at[k], out_ref.at[:, quantum(k), :], sems.at[1, k])

    def out_last():
        yield pltpu.make_async_copy(cells_buf.at[total - 1], last_ref, more_sems.at[5])
        yield pltpu.make_async_copy(half_buf, half_ref, more_sems.at[6])
        yield pltpu.make_async_copy(raw_buf.at[pl.ds(0, split)], top_ref, more_sems.at[7])
        yield pltpu.make_async_copy(raw_buf.at[pl.ds(split, SPAN - split)], bottom_ref, more_sems.at[8])

    copies = [
        pltpu.make_async_copy(g_ref.at[rows_of(slot), quantum(total - 1), :], g_buf, more_sems.at[9]),
        pltpu.make_async_copy(r_ref.at[:, quantum(r_ref.shape[1] // QUANTUM - 1), :], r_buf, more_sems.at[10]),
        pltpu.make_async_copy(bands_ref, band_buf, more_sems.at[11]),
    ]
    for copy in copies:
        copy.start()
    consts = load(constants, buffers, more_sems)
    for k in range(total):
        into(k).start()
    for copy in (*copies, *consts):
        copy.wait()
    rows, kept, low_back, band, band_back = buffers

    theirs = g_buf[...].astype(jnp.float32) + r_buf[...]
    c = []
    for s, x in enumerate(beside(theirs)):
        c.append(dot(rows[...] if s < 2 else rows[:BAND, :], tall(x)))
    for k in range(GROUP):
        half_buf[k * HIGH : (k + 1) * HIGH, :] = c[k // 4][BAND:, k % 4 * LANES : (k % 4 + 1) * LANES]
    w = dot(long(jnp.concatenate([c[0][:BAND], c[1][:BAND]], axis=0)), kept[...])
    for i in range(3):
        at = GROUP * HIGH + i * QUARTER
        half_buf[at : at + QUARTER, :] = w[:, i * LANES : (i + 1) * LANES]
    theirs_band = dot(long(jnp.concatenate(c[2:], axis=0)), band[...])
    b = jnp.concatenate([band_buf[...].reshape(total * SPAN, LANES), theirs_band], axis=0)
    wide = dot(long(b), band_back[...])
    low_buf[...] = wide[: total * SPAN].reshape(total, SPAN, 4 * LANES)
    low = wide[total * SPAN :]
    raw_buf[...] = theirs[:, GROUP:, :] - back([low[:BAND], low[BAND:]], low_back[...])

    def body(k, _):
        into(k).wait()
        turned = lax.rem(k + total - lax.div(own_turn, 2), total)
        cells_buf[k] = cells_buf[k] - back(bands_of(low_buf[turned]), low_back[...])

        @pl.when(k < total - 1)
        def _():
            out(k).start()

        return 0

    lax.fori_loop(0, total, body, 0)
    for copy in out_last():
        copy.start()
    for k in range(total - 1):
        out(k).wait()
    for copy in out_last():
        copy.wait()


def decode_kernel(first, count, pay_ref, rows_back, kept_back, base_ref, out_ref, *refs):
    pay_buf, base_buf, low_buf, rows_buf, kept_buf, sems, const_sems = refs
    at = QUANTUM * HIGH

    def into(k):
        yield pltpu.make_async_copy(pay_ref.at[k], pay_buf.at[k], sems.at[0, k])
        yield pltpu.make_async_copy(base_ref.at[:, quantum(first + k), :], base_buf.at[k], sems.at[1, k])

    def out(k):
        return pltpu.make_async_copy(base_buf.at[k], out_ref.at[:, quantum(first + k), :], sems.at[2, k])

    for k in range(count):
        for copy in into(k):
            copy.start()
    for copy in load((rows_back, kept_back), (rows_buf, kept_buf), const_sems):
        copy.wait()
    for k in range(count):
        for copy in into(k):
            copy.wait()
    kept = [
        jnp.concatenate([pay_buf[k, at + i * SPAN : at + (i + 1) * SPAN, :] for i in range(3)], axis=1)
        for k in range(count)
    ]
    low_buf[...] = dot(long(jnp.concatenate(kept, axis=0)), kept_buf[...]).reshape(count, SPAN, 4 * LANES)

    def body(k, _):
        parts = []
        for s, low in enumerate(bands_of(low_buf[k])):
            high = [pay_buf[k, (4 * s + j) * HIGH : (4 * s + j + 1) * HIGH, :] for j in range(4)]
            parts.append(jnp.concatenate([low, jnp.concatenate(high, axis=1)], axis=0))
        base_buf[k] = base_buf[k] + back(parts, rows_buf[...])
        out(k).start()
        return 0

    lax.fori_loop(0, count, body, 0)
    for k in range(count):
        out(k).wait()


def add_kernel(first, row, there_ref, last_ref, base_ref, out_ref, sum_buf, sem):
    rows = pl.ds(row, there_ref.shape[0])
    sum_buf[...] = last_ref[rows, GROUP:, :] + there_ref[...]
    out = pltpu.make_async_copy(sum_buf, out_ref.at[rows, pl.ds(first * QUANTUM + GROUP, GROUP)], sem.at[0])
    out.start()
    out.wait()


def half_kernel(first, half_ref, last_ref, rows_back, kept_back, base_ref, out_ref, sum_buf, sem):
    at = GROUP * HIGH
    w = jnp.concatenate([half_ref[at + i * QUARTER : at + (i + 1) * QUARTER, :] for i in range(3)], axis=1)
    low = dot(long(w), kept_back[...])
    parts = []
    for s in range(2):
        high = [half_ref[k * HIGH : (k + 1) * HIGH, :] for k in range(4 * s, 4 * s + 4)]
        parts.append(jnp.concatenate([low[s * BAND : (s + 1) * BAND], jnp.concatenate(high, axis=1)], axis=0))
    sum_buf[...] = last_ref[:, :GROUP, :] + back(parts, rows_back[...])
    out = pltpu.make_async_copy(sum_buf, out_ref.at[:, pl.ds(first * QUANTUM, GROUP)], sem.at[0])
    out.start()
    out.wait()


def update_kernel(scale, count, place, band_ref, low_back, band_back, out_ref, band_buf, low_rows, back_buf, out_buf, low_buf, sems, const_sems):
    own_turn = turn()
    for copy in load((band_ref, low_back, band_back), (band_buf, low_rows, back_buf), const_sems):
        copy.wait()
    b = band_buf[...].reshape(count * SPAN, LANES) * scale
    low_buf[...] = dot(long(b), back_buf[...]).reshape(count, SPAN, 4 * LANES)

    def out(k):
        return pltpu.make_async_copy(out_buf.at[k], out_ref.at[:, quantum(k), :], sems.at[k])

    def body(k, _):
        turned = lax.rem(k + count - lax.div(own_turn, 2), count)
        out_buf[k] = back(bands_of(low_buf[turned]), low_rows[...])
        out(k).start()
        return 0

    lax.fori_loop(0, count, body, 0)
    for k in range(count):
        out(k).wait()


ANY = pl.BlockSpec(memory_space=pl.ANY)
BANDS = jax.ShapeDtypeStruct((PLANE, QUARTER, LANES), jnp.float32)


def call(kernel, place, operands, outs, scratch, aliases, vmem, near=0):
    operands = operands if place is None else [place, *operands]
    return pl.pallas_call(
        kernel,
        grid_spec=pltpu.PrefetchScalarGridSpec(
            num_scalar_prefetch=0,
            grid=(),
            in_specs=[pl.BlockSpec(memory_space=pltpu.VMEM)] * near + [ANY] * (len(operands) - near),
            out_specs=[ANY] * len(outs),
            scratch_shapes=scratch,
        ),
        out_shape=outs,
        input_output_aliases=aliases,
        cost_estimate=pl.CostEstimate(flops=0, bytes_accessed=0, transcendentals=0),
        compiler_params=pltpu.CompilerParams(vmem_limit_bytes=vmem * 1024 * 1024),
    )(*operands)


def floats(*shape):
    return jax.ShapeDtypeStruct(shape, jnp.float32)


def held(count, *dtypes):
    return [pltpu.VMEM((count, SPAN, QUANTUM, LANES), dtype) for dtype in dtypes]


def lows(count):
    return [pltpu.VMEM((count, SPAN, 4 * LANES), jnp.float32)]


def same(arrays):
    return [pltpu.VMEM(a.shape, a.dtype) for a in arrays]


def sems(*shape):
    return pltpu.SemaphoreType.DMA(shape)


def cast(place, g, *wanted):
    n = sum(count for _, _, count in wanted)
    return call(
        functools.partial(cast_kernel, wanted),
        place,
        [g],
        [floats(SPAN, count * QUANTUM, LANES) for _, _, count in wanted],
        held(n, jnp.bfloat16, jnp.float32) + [sems(2, n)],
        {},
        MOST,
    )


def encoded(place, g, received, first, counts, slot, mats, bands=None):
    values = [mats["rows"], mats["lanes"]]
    extra = int(bands is not None)
    sent = sum(counts)
    n = sent + extra
    return call(
        functools.partial(encode_kernel, first, counts, extra, slot, [r.shape[1] // QUANTUM for r in received]),
        place,
        [g, *received, *values, *([bands] * extra)],
        [floats(c, PAYLOAD, LANES) for c in counts] + [BANDS],
        held(n, jnp.bfloat16, jnp.float32)
        + [pltpu.VMEM((sent, PAYLOAD, LANES), jnp.float32), pltpu.VMEM((n, 2, QUARTER, LANES), jnp.float32)]
        + lows(n)
        + [pltpu.VMEM((2, QUARTER, LANES), jnp.float32)]
        + same(values)
        + [sems(5, n), sems(3)],
        {4 + len(received): len(counts)} if extra else {},
        MOST,
    )


def moments(place, m, g, early, received, slot, mats):
    values = [mats["low"], mats["band"]]
    counts = [r.shape[1] // QUANTUM for r in received]
    n = sum(counts)
    return call(
        functools.partial(moment_kernel, counts, slot),
        place,
        [m, g, early, *received, *values],
        [floats(*m.shape), BANDS],
        held(n, jnp.float32, jnp.bfloat16, jnp.float32)
        + [pltpu.VMEM((n, 2, QUARTER, LANES), jnp.float32)]
        + lows(n)
        + [pltpu.VMEM((SPAN, QUANTUM, LANES), jnp.float32)]
        + same(values)
        + [sems(5, n), sems(3)],
        {},
        MOST,
    )


def rest(place, cells, bands, g, received, slot, mats):
    values = [mats[name] for name in ("rows", "kept", "low_back", "band", "band_back")]
    n = cells.shape[1] // QUANTUM
    half = (GROUP * HIGH + 3 * QUARTER, LANES)
    return call(
        functools.partial(rest_kernel, slot),
        place,
        [cells, bands, g, received, *values],
        [
            floats(*cells.shape),
            floats(SPAN, QUANTUM, LANES),
            floats(*half),
            floats(SPLIT, GROUP, LANES),
            floats(SPAN - SPLIT, GROUP, LANES),
        ],
        held(n, jnp.float32)
        + [pltpu.VMEM(BANDS.shape, jnp.float32)]
        + lows(n)
        + [pltpu.VMEM((SPAN, QUANTUM, LANES), dtype) for dtype in (jnp.bfloat16, jnp.float32)]
        + [pltpu.VMEM(half, jnp.float32), pltpu.VMEM((SPAN, GROUP, LANES), jnp.float32)]
        + same(values)
        + [sems(2, n), sems(12)],
        {1: 0},
        MOST,
    )


def added(there, last, base, first, row):
    return call(
        functools.partial(add_kernel, first, row),
        None,
        [there, last, base],
        [floats(*base.shape)],
        same([there]) + [sems(1)],
        {2: 0},
        MOST,
        2,
    )[0]


def added_half(there, last, base, first, mats):
    return call(
        functools.partial(half_kernel, first),
        None,
        [there, last, mats["rows_back"], mats["kept_back"], base],
        [floats(*base.shape)],
        [pltpu.VMEM((SPAN, GROUP, LANES), jnp.float32), sems(1)],
        {4: 0},
        MOST,
        4,
    )[0]


def decoded(payload, base, first, mats):
    values = [mats["rows_back"], mats["kept_back"]]
    count = payload.shape[0]
    return call(
        functools.partial(decode_kernel, first, count),
        None,
        [payload, *values, base],
        [floats(*base.shape)],
        [pltpu.VMEM((count, PAYLOAD, LANES), jnp.float32)]
        + held(count, jnp.float32)
        + lows(count)
        + same(values)
        + [sems(3, count), sems(2)],
        {3: 0},
        MOST,
    )[0]


def updated(place, band, scale, shape, mats):
    values = [mats["low_back"], mats["band_back"]]
    count = shape[1] // QUANTUM
    return call(
        functools.partial(update_kernel, scale, count),
        place,
        [band, *values],
        [floats(*shape)],
        same([band, *values]) + held(count, jnp.float32) + lows(count) + [sems(count), sems(3)],
        {},
        MOST,
    )[0]


def tiles(x):
    rows, mats, width = x.shape
    x = x.reshape(rows, mats, width // LANES, LANES).transpose(0, 2, 1, 3)
    return x.reshape(rows, mats * width // LANES, LANES)


def untiles(x, mats):
    rows, places, _ = x.shape
    x = x.reshape(rows, places // mats, mats, LANES).transpose(0, 2, 1, 3)
    return x.reshape(rows, mats, places // mats * LANES)


def tie(*arrays):
    return lax.optimization_barrier(arrays)


def per_device(grads, momentum):
    rep_count = lax.axis_size("rep")
    mat_count = grads.shape[3]
    mats = constants()
    g = tiles(grads[0, 0])
    m = tiles(momentum[0])
    count = m.shape[1] // QUANTUM
    member = lax.axis_index("fsdp")
    place = jnp.full((8, LANES), member, jnp.int32)
    over_core = [(f, f ^ 1) for f in range(4)]
    over_z = [(f, f ^ 2) for f in range(4)]

    def core(x):
        return lax.ppermute(x, "fsdp", over_core)

    def link(x):
        return lax.ppermute(x, "fsdp", over_z)

    def head(slot):
        return lax.dynamic_slice(g, ((member ^ slot) * SPAN, 0, 0), (SPAN, QUANTUM, LANES)).astype(jnp.float32)

    place1, cells = tie(place, head(3))
    more, own = cast(place1, g, (3, 1, SECOND), (2, 0, 1))
    got, more = tie(core(cells), more)
    cells = own + got
    early = link(cells)
    pay, other_band = encoded(place, g, [core(more)], 1, (SECOND,), 2, mats)
    second = link(pay)
    place2, _ = tie(place1, pay)
    wanted = [(3, k, 1) for k in range(1 + SECOND, count)] + [(1, k, 2) for k in range(0, count, 2)]
    *cells, later = cast(place2, g, *wanted)
    early, later, _ = tie(early, later, pay)
    pieces = [core(c) for c in [*cells, later]]
    got, mine = pieces[: -count // 2], pieces[-count // 2 :]
    pay, other_band = encoded(place, g, got, 1 + SECOND, (count - 2 - SECOND,), 2, mats, other_band)
    third = link(pay)
    names = ("rep", "fsdp")
    wrapped = lax.ppermute(other_band, names, steps(rep_count, 0, 2))
    cells, own_band = moments(place, m, g, early, mine, 0, mats)
    base, last, half, top, bottom = rest(place, cells, own_band, g, got[-1], 2, mats)

    groups = [[h * PLANE + i for i in range(PLANE)] for h in range(rep_count // PLANE)]
    met = lax.all_to_all(own_band + wrapped, "rep", 0, 0, axis_index_groups=groups, tiled=True)
    met, bottom = tie(met, bottom)
    half, top, bottom = link(half), link(top), link(bottom)
    part = jnp.sum(met.reshape(PLANE, QUARTER, LANES), axis=0)
    total = part + lax.ppermute(part, names, steps(rep_count, TURN, 0))
    total, second = tie(total, second)
    spread = jnp.broadcast_to(total[None], (PLANE,) + total.shape)
    band_total = lax.all_to_all(spread, "rep", 0, 0, axis_index_groups=groups, tiled=True)
    out, band_total = tie(decoded(second, base, 1, mats), band_total)
    update = updated(place, band_total, 1.0 / rep_count, m.shape, mats)

    third, update = tie(third, update)
    out = decoded(third, out, 1 + SECOND, mats)
    half, out = tie(half, out)
    out = added_half(half, last, out, count - 1, mats)
    top, out = tie(top, out)
    out = added(top, last, out, count - 1, 0)
    bottom, out = tie(bottom, out)
    out = added(bottom, last, out, count - 1, SPLIT)
    return (untiles(out, mat_count)[None], untiles(update, mat_count))


def steps(rep_count, turn, member):
    pairs = []
    for rep in range(rep_count):
        high, low = divmod(rep, PLANE)
        to = (high ^ 1) * PLANE + (low + (turn if high else PLANE - turn)) % PLANE
        pairs += [(rep * 4 + f, to * 4 + (f ^ member)) for f in range(4)]
    return pairs


def solution(mesh):
    in_specs = (P("rep", "fsdp", None, None, None), P("rep", "fsdp", None, None))
    out_specs = (P("rep", "fsdp", None, None), P("fsdp", None, None))
    return jax.shard_map(
        per_device, mesh=mesh, in_specs=in_specs, out_specs=out_specs, check_vma=False
    )
```

```python
import functools
import math

import jax
import jax.numpy as jnp
import ml_dtypes
import numpy as np
from jax import lax
from jax.experimental import pallas as pl
from jax.experimental.pallas import tpu as pltpu
from jax.sharding import PartitionSpec as P

SPAN = 64
BAND = 16
LANES = 128
GROUP = 8
QUANTUM = 2 * GROUP
DECAY = 0.9
HIGH = SPAN - BAND
QUARTER = GROUP // 4 * BAND
PAYLOAD = QUANTUM * HIGH + 3 * SPAN
SECOND = 4
SPLIT = 48
PLANE = 16
TURN = 4
MOST = 46


def dct(order):
    q = np.arange(order)[:, None]
    n = np.arange(order)[None, :]
    scale = np.where(q == 0, math.sqrt(1.0 / order), math.sqrt(2.0 / order))
    return scale * np.cos(math.pi * (2 * n + 1) * q / (2 * order))


def halves(a):
    high = a.astype(ml_dtypes.bfloat16)
    return high, (a - high.astype(np.float64)).astype(ml_dtypes.bfloat16)


def left(a):
    high, low = halves(a)
    return np.concatenate([high, low, high], axis=1)


def right(a):
    high, low = halves(a)
    return np.concatenate([high, low, high], axis=0)


def constants():
    t = dct(SPAN)
    lanes = np.kron(np.eye(8), t.T)
    coef = np.arange(512) % SPAN
    order = np.concatenate([np.flatnonzero(coef >= BAND), np.flatnonzero(coef < BAND)])
    lanes = lanes[:, order]
    kept, band = lanes[:, : 3 * LANES], lanes[:, 3 * LANES :]
    mats = dict(
        rows=left(t), rows_back=left(t.T), low=left(t[:BAND]), low_back=left(t[:BAND].T),
        lanes=right(lanes), kept=right(kept), kept_back=right(kept.T), band=right(band), band_back=right(band.T),
    )
    return {name: jnp.asarray(a) for name, a in mats.items()}


def split(x):
    high = x.astype(jnp.bfloat16)
    return high, (x - high.astype(jnp.float32)).astype(jnp.bfloat16)


def tall(x):
    high, low = split(x)
    return jnp.concatenate([high, high, low], axis=0)


def long(x):
    high, low = split(x)
    return jnp.concatenate([high, high, low], axis=1)


def dot(a, b):
    return jnp.dot(a, b, preferred_element_type=jnp.float32)


def beside(x):
    x = jnp.swapaxes(x, 0, 1)
    return [jnp.concatenate([x[4 * s + j] for j in range(4)], axis=1) for s in range(4)]


def apart(parts):
    x = jnp.stack([p[:, j * LANES : (j + 1) * LANES] for p in parts for j in range(4)], axis=0)
    return jnp.swapaxes(x, 0, 1)


def forward(x, rows):
    return [dot(rows, tall(part)) for part in beside(x)]


def back(parts, rows):
    return apart([dot(rows, tall(p)) for p in parts])


def bands_of(c):
    return [c[s * BAND : (s + 1) * BAND] for s in range(4)]


def rows_of(slot):
    member = lax.axis_index("fsdp") ^ slot
    return pl.ds(pl.multiple_of(member * SPAN, SPAN), SPAN)


def turn(other=False):
    own = lax.div(lax.axis_index("rep"), PLANE) * TURN
    return TURN - own if other else own


def quantum(k):
    return pl.ds(k * QUANTUM, QUANTUM)


def band_at(k, shift):
    return pl.ds(lax.rem(2 * k + PLANE - shift, PLANE), 2)


def load(constants, buffers, sems):
    copies = [pltpu.make_async_copy(c, b, sems.at[i]) for i, (c, b) in enumerate(zip(constants, buffers))]
    for copy in copies:
        copy.start()
    return copies


def cast_kernel(wanted, place, g_ref, *refs):
    outs, (held, cells, sems) = refs[: len(wanted)], refs[len(wanted) :]
    into, out = [], []
    for o, (slot, first, n) in zip(outs, wanted):
        for j in range(n):
            k = len(into)
            source = g_ref.at[rows_of(slot), quantum(first + j), :]
            into.append(pltpu.make_async_copy(source, held.at[k], sems.at[0, k]))
            out.append(pltpu.make_async_copy(cells.at[k], o.at[:, quantum(j), :], sems.at[1, k]))
            into[-1].start()
    for k in range(len(into)):
        into[k].wait()
        cells[k] = held[k].astype(jnp.float32)
        out[k].start()
    for copy in out:
        copy.wait()


def encode_kernel(first, counts, extra, slot, received, place, g_ref, *refs):
    come = [(ref, j) for ref, n in zip(refs, received) for j in range(n)]
    rows, lanes, *refs = refs[len(received) :]
    refs = refs[extra:]
    pays, refs = refs[: len(counts)], refs[len(counts) :]
    band_ref, g_buf, r_buf, pay_buf, band_buf, low_buf, zero_buf, rows_buf, lanes_buf, sems, more_sems = refs
    high = QUANTUM * HIGH
    sent = sum(counts)
    count = sent + extra
    where = [(ref, j) for ref, n in zip(pays, counts) for j in range(n)]
    other_turn = turn(other=True)

    def into(k, ref=None, j=0):
        ref = come[0][0] if ref is None else ref
        yield pltpu.make_async_copy(g_ref.at[rows_of(slot), quantum(first + k), :], g_buf.at[k], sems.at[0, k])
        yield pltpu.make_async_copy(ref.at[:, quantum(j), :], r_buf.at[k], sems.at[1, k])

    def out_high(k, ref, j):
        at = pl.ds(0, high)
        return pltpu.make_async_copy(pay_buf.at[k, at], ref.at[j, at], sems.at[2, k])

    def out_low(k, ref, j):
        at = pl.ds(high, 3 * SPAN)
        return pltpu.make_async_copy(pay_buf.at[k, at], ref.at[j, at], sems.at[3, k])

    def out_band(k):
        return pltpu.make_async_copy(band_buf.at[k], band_ref.at[band_at(first + k, other_turn)], sems.at[4, k])

    if not extra:
        blank = pltpu.make_async_copy(zero_buf, band_ref.at[band_at(0, other_turn)], more_sems.at[2])
    for copy in into(0, *come[0]):
        copy.start()
    consts = load((rows, lanes), (rows_buf, lanes_buf), more_sems)
    for k in range(1, count):
        for copy in into(k, *come[k]):
            copy.start()
    if not extra:
        zero_buf[...] = jnp.zeros_like(zero_buf)
        blank.start()
    consts[0].wait()

    def low_of(k, c, s):
        low_buf[k, s * BAND : (s + 1) * BAND, :] = c[:BAND]

    def cells_of(k):
        for copy in into(k):
            copy.wait()
        return g_buf[k].astype(jnp.float32) + r_buf[k]

    def body(k, _):
        for s, c in enumerate(forward(cells_of(k), rows_buf[...])):
            low_of(k, c, s)
            for j in range(4):
                at = (4 * s + j) * HIGH
                pay_buf[k, at : at + HIGH, :] = c[BAND:, j * LANES : (j + 1) * LANES]
        for i, ref in enumerate(pays):
            start = sum(counts[:i])

            @pl.when((k >= start) & (k < start + counts[i]))
            def _():
                out_high(k, ref, k - start).start()

        return 0

    lax.fori_loop(0, sent, body, 0)
    for k in range(sent, count):
        for s, c in enumerate(forward(cells_of(k), rows_buf[:BAND, :])):
            low_of(k, c, s)
    consts[1].wait()
    w = dot(long(low_buf[...].reshape(count * SPAN, 4 * LANES)), lanes_buf[...])
    for k in range(count):
        part = w[k * SPAN : (k + 1) * SPAN]
        if k < sent:
            for i in range(3):
                at = high + i * SPAN
                pay_buf[k, at : at + SPAN, :] = part[:, i * LANES : (i + 1) * LANES]
            out_low(k, *where[k]).start()
        band_buf[k] = part[:, 3 * LANES :].reshape(2, QUARTER, LANES)
        out_band(k).start()
    for k in range(count):
        if k < sent:
            out_high(k, *where[k]).wait()
            out_low(k, *where[k]).wait()
        out_band(k).wait()
    if not extra:
        blank.wait()


def moment_kernel(counts, slot, place, m_ref, g_ref, early_ref, *refs):
    received, refs = refs[: len(counts)], refs[len(counts) :]
    constants, refs = refs[:2], refs[2:]
    cells_ref, band_ref, m_buf, g_buf, r_buf, band_buf, low_buf, early_buf = refs[:8]
    buffers, (sems, more_sems) = refs[8:10], refs[10:]
    own_turn = turn()
    total = sum(counts)
    where = [(r, j) for r, n in zip(received, counts) for j in range(n)]

    def into(k, r=None, j=0):
        r = received[0] if r is None else r
        yield pltpu.make_async_copy(g_ref.at[rows_of(slot), quantum(k), :], g_buf.at[k], sems.at[0, k])
        yield pltpu.make_async_copy(r.at[:, quantum(j), :], r_buf.at[k], sems.at[1, k])
        yield pltpu.make_async_copy(m_ref.at[:, quantum(k), :], m_buf.at[k], sems.at[2, k])

    def out(k):
        return pltpu.make_async_copy(m_buf.at[k], cells_ref.at[:, quantum(k), :], sems.at[3, k])

    def out_band(k):
        return pltpu.make_async_copy(band_buf.at[k], band_ref.at[band_at(k, own_turn)], sems.at[4, k])

    early = pltpu.make_async_copy(early_ref, early_buf, more_sems.at[2])
    for copy in (*into(0, *where[0]), early):
        copy.start()
    consts = load(constants, buffers, more_sems)
    for k in range(1, total):
        for copy in into(k, *where[k]):
            copy.start()
    for copy in consts:
        copy.wait()
    low, band = buffers

    def cells_of(k, more=None):
        for copy in into(k):
            copy.wait()
        cells = DECAY * m_buf[k] + (g_buf[k].astype(jnp.float32) + r_buf[k])
        if more is not None:
            cells = cells + more
        m_buf[k] = cells
        out(k).start()
        for s, c in enumerate(forward(cells, low[...])):
            low_buf[k, s * BAND : (s + 1) * BAND, :] = c

    def body(k, _):
        cells_of(k)
        return 0

    early.wait()
    cells_of(0, early_buf[...])
    lax.fori_loop(1, total, body, 0)
    b = dot(long(low_buf[...].reshape(total * SPAN, 4 * LANES)), band[...])
    band_buf[...] = b.reshape(total, 2, QUARTER, LANES)
    for k in range(total):
        out_band(k).start()
    for k in range(total):
        out(k).wait()
        out_band(k).wait()


def rest_kernel(slot, place, cells_ref, bands_ref, g_ref, r_ref, *refs):
    constants, refs = refs[:5], refs[5:]
    out_ref, last_ref, half_ref, top_ref, bottom_ref = refs[:5]
    cells_buf, band_buf, low_buf, g_buf, r_buf, half_buf, raw_buf = refs[5:12]
    buffers, (sems, more_sems) = refs[12:17], refs[17:]
    own_turn = turn()
    total = cells_buf.shape[0]
    split = top_ref.shape[0]

    def into(k):
        return pltpu.make_async_copy(cells_ref.at[:, quantum(k), :], cells_buf.at[k], sems.at[0, k])

    def out(k):
        return pltpu.make_async_copy(cells_buf.at[k], out_ref.at[:, quantum(k), :], sems.at[1, k])

    def out_last():
        yield pltpu.make_async_copy(cells_buf.at[total - 1], last_ref, more_sems.at[5])
        yield pltpu.make_async_copy(half_buf, half_ref, more_sems.at[6])
        yield pltpu.make_async_copy(raw_buf.at[pl.ds(0, split)], top_ref, more_sems.at[7])
        yield pltpu.make_async_copy(raw_buf.at[pl.ds(split, SPAN - split)], bottom_ref, more_sems.at[8])

    copies = [
        pltpu.make_async_copy(g_ref.at[rows_of(slot), quantum(total - 1), :], g_buf, more_sems.at[9]),
        pltpu.make_async_copy(r_ref.at[:, quantum(r_ref.shape[1] // QUANTUM - 1), :], r_buf, more_sems.at[10]),
        pltpu.make_async_copy(bands_ref, band_buf, more_sems.at[11]),
    ]
    for copy in copies:
        copy.start()
    consts = load(constants, buffers, more_sems)
    for k in range(total):
        into(k).start()
    for copy in (*copies, *consts):
        copy.wait()
    rows, kept, low_back, band, band_back = buffers

    theirs = g_buf[...].astype(jnp.float32) + r_buf[...]
    c = []
    for s, x in enumerate(beside(theirs)):
        c.append(dot(rows[...] if s < 2 else rows[:BAND, :], tall(x)))
    for k in range(GROUP):
        half_buf[k * HIGH : (k + 1) * HIGH, :] = c[k // 4][BAND:, k % 4 * LANES : (k % 4 + 1) * LANES]
    w = dot(long(jnp.concatenate([c[0][:BAND], c[1][:BAND]], axis=0)), kept[...])
    for i in range(3):
        at = GROUP * HIGH + i * QUARTER
        half_buf[at : at + QUARTER, :] = w[:, i * LANES : (i + 1) * LANES]
    theirs_band = dot(long(jnp.concatenate(c[2:], axis=0)), band[...])
    b = jnp.concatenate([band_buf[...].reshape(total * SPAN, LANES), theirs_band], axis=0)
    wide = dot(long(b), band_back[...])
    low_buf[...] = wide[: total * SPAN].reshape(total, SPAN, 4 * LANES)
    low = wide[total * SPAN :]
    raw_buf[...] = theirs[:, GROUP:, :] - back([low[:BAND], low[BAND:]], low_back[...])

    def body(k, _):
        into(k).wait()
        turned = lax.rem(k + total - lax.div(own_turn, 2), total)
        cells_buf[k] = cells_buf[k] - back(bands_of(low_buf[turned]), low_back[...])

        @pl.when(k < total - 1)
        def _():
            out(k).start()

        return 0

    lax.fori_loop(0, total, body, 0)
    for copy in out_last():
        copy.start()
    for k in range(total - 1):
        out(k).wait()
    for copy in out_last():
        copy.wait()


def decode_kernel(first, count, pay_ref, rows_back, kept_back, base_ref, out_ref, *refs):
    pay_buf, base_buf, low_buf, rows_buf, kept_buf, sems, const_sems = refs
    at = QUANTUM * HIGH

    def into(k):
        yield pltpu.make_async_copy(pay_ref.at[k], pay_buf.at[k], sems.at[0, k])
        yield pltpu.make_async_copy(base_ref.at[:, quantum(first + k), :], base_buf.at[k], sems.at[1, k])

    def out(k):
        return pltpu.make_async_copy(base_buf.at[k], out_ref.at[:, quantum(first + k), :], sems.at[2, k])

    for k in range(count):
        for copy in into(k):
            copy.start()
    for copy in load((rows_back, kept_back), (rows_buf, kept_buf), const_sems):
        copy.wait()
    for k in range(count):
        for copy in into(k):
            copy.wait()
    kept = [
        jnp.concatenate([pay_buf[k, at + i * SPAN : at + (i + 1) * SPAN, :] for i in range(3)], axis=1)
        for k in range(count)
    ]
    low_buf[...] = dot(long(jnp.concatenate(kept, axis=0)), kept_buf[...]).reshape(count, SPAN, 4 * LANES)

    def body(k, _):
        parts = []
        for s, low in enumerate(bands_of(low_buf[k])):
            high = [pay_buf[k, (4 * s + j) * HIGH : (4 * s + j + 1) * HIGH, :] for j in range(4)]
            parts.append(jnp.concatenate([low, jnp.concatenate(high, axis=1)], axis=0))
        base_buf[k] = base_buf[k] + back(parts, rows_buf[...])
        out(k).start()
        return 0

    lax.fori_loop(0, count, body, 0)
    for k in range(count):
        out(k).wait()


def add_kernel(first, row, there_ref, last_ref, base_ref, out_ref, sum_buf, sem):
    rows = pl.ds(row, there_ref.shape[0])
    sum_buf[...] = last_ref[rows, GROUP:, :] + there_ref[...]
    out = pltpu.make_async_copy(sum_buf, out_ref.at[rows, pl.ds(first * QUANTUM + GROUP, GROUP)], sem.at[0])
    out.start()
    out.wait()


def half_kernel(first, half_ref, last_ref, rows_back, kept_back, base_ref, out_ref, sum_buf, sem):
    at = GROUP * HIGH
    w = jnp.concatenate([half_ref[at + i * QUARTER : at + (i + 1) * QUARTER, :] for i in range(3)], axis=1)
    low = dot(long(w), kept_back[...])
    parts = []
    for s in range(2):
        high = [half_ref[k * HIGH : (k + 1) * HIGH, :] for k in range(4 * s, 4 * s + 4)]
        parts.append(jnp.concatenate([low[s * BAND : (s + 1) * BAND], jnp.concatenate(high, axis=1)], axis=0))
    sum_buf[...] = last_ref[:, :GROUP, :] + back(parts, rows_back[...])
    out = pltpu.make_async_copy(sum_buf, out_ref.at[:, pl.ds(first * QUANTUM, GROUP)], sem.at[0])
    out.start()
    out.wait()


def update_kernel(scale, count, place, band_ref, low_back, band_back, out_ref, band_buf, low_rows, back_buf, out_buf, low_buf, sems, const_sems):
    own_turn = turn()
    for copy in load((band_ref, low_back, band_back), (band_buf, low_rows, back_buf), const_sems):
        copy.wait()
    b = band_buf[...].reshape(count * SPAN, LANES) * scale
    low_buf[...] = dot(long(b), back_buf[...]).reshape(count, SPAN, 4 * LANES)

    def out(k):
        return pltpu.make_async_copy(out_buf.at[k], out_ref.at[:, quantum(k), :], sems.at[k])

    def body(k, _):
        turned = lax.rem(k + count - lax.div(own_turn, 2), count)
        out_buf[k] = back(bands_of(low_buf[turned]), low_rows[...])
        out(k).start()
        return 0

    lax.fori_loop(0, count, body, 0)
    for k in range(count):
        out(k).wait()


ANY = pl.BlockSpec(memory_space=pl.ANY)
BANDS = jax.ShapeDtypeStruct((PLANE, QUARTER, LANES), jnp.float32)


def call(kernel, place, operands, outs, scratch, aliases, vmem, near=0):
    operands = operands if place is None else [place, *operands]
    return pl.pallas_call(
        kernel,
        grid_spec=pltpu.PrefetchScalarGridSpec(
            num_scalar_prefetch=0,
            grid=(),
            in_specs=[pl.BlockSpec(memory_space=pltpu.VMEM)] * near + [ANY] * (len(operands) - near),
            out_specs=[ANY] * len(outs),
            scratch_shapes=scratch,
        ),
        out_shape=outs,
        input_output_aliases=aliases,
        cost_estimate=pl.CostEstimate(flops=0, bytes_accessed=0, transcendentals=0),
        compiler_params=pltpu.CompilerParams(vmem_limit_bytes=vmem * 1024 * 1024),
    )(*operands)


def floats(*shape):
    return jax.ShapeDtypeStruct(shape, jnp.float32)


def held(count, *dtypes):
    return [pltpu.VMEM((count, SPAN, QUANTUM, LANES), dtype) for dtype in dtypes]


def lows(count):
    return [pltpu.VMEM((count, SPAN, 4 * LANES), jnp.float32)]


def same(arrays):
    return [pltpu.VMEM(a.shape, a.dtype) for a in arrays]


def sems(*shape):
    return pltpu.SemaphoreType.DMA(shape)


def cast(place, g, *wanted):
    n = sum(count for _, _, count in wanted)
    return call(
        functools.partial(cast_kernel, wanted),
        place,
        [g],
        [floats(SPAN, count * QUANTUM, LANES) for _, _, count in wanted],
        held(n, jnp.bfloat16, jnp.float32) + [sems(2, n)],
        {},
        MOST,
    )


def encoded(place, g, received, first, counts, slot, mats, bands=None):
    values = [mats["rows"], mats["lanes"]]
    extra = int(bands is not None)
    sent = sum(counts)
    n = sent + extra
    return call(
        functools.partial(encode_kernel, first, counts, extra, slot, [r.shape[1] // QUANTUM for r in received]),
        place,
        [g, *received, *values, *([bands] * extra)],
        [floats(c, PAYLOAD, LANES) for c in counts] + [BANDS],
        held(n, jnp.bfloat16, jnp.float32)
        + [pltpu.VMEM((sent, PAYLOAD, LANES), jnp.float32), pltpu.VMEM((n, 2, QUARTER, LANES), jnp.float32)]
        + lows(n)
        + [pltpu.VMEM((2, QUARTER, LANES), jnp.float32)]
        + same(values)
        + [sems(5, n), sems(3)],
        {4 + len(received): len(counts)} if extra else {},
        MOST,
    )


def moments(place, m, g, early, received, slot, mats):
    values = [mats["low"], mats["band"]]
    counts = [r.shape[1] // QUANTUM for r in received]
    n = sum(counts)
    return call(
        functools.partial(moment_kernel, counts, slot),
        place,
        [m, g, early, *received, *values],
        [floats(*m.shape), BANDS],
        held(n, jnp.float32, jnp.bfloat16, jnp.float32)
        + [pltpu.VMEM((n, 2, QUARTER, LANES), jnp.float32)]
        + lows(n)
        + [pltpu.VMEM((SPAN, QUANTUM, LANES), jnp.float32)]
        + same(values)
        + [sems(5, n), sems(3)],
        {},
        MOST,
    )


def rest(place, cells, bands, g, received, slot, mats):
    values = [mats[name] for name in ("rows", "kept", "low_back", "band", "band_back")]
    n = cells.shape[1] // QUANTUM
    half = (GROUP * HIGH + 3 * QUARTER, LANES)
    return call(
        functools.partial(rest_kernel, slot),
        place,
        [cells, bands, g, received, *values],
        [
            floats(*cells.shape),
            floats(SPAN, QUANTUM, LANES),
            floats(*half),
            floats(SPLIT, GROUP, LANES),
            floats(SPAN - SPLIT, GROUP, LANES),
        ],
        held(n, jnp.float32)
        + [pltpu.VMEM(BANDS.shape, jnp.float32)]
        + lows(n)
        + [pltpu.VMEM((SPAN, QUANTUM, LANES), dtype) for dtype in (jnp.bfloat16, jnp.float32)]
        + [pltpu.VMEM(half, jnp.float32), pltpu.VMEM((SPAN, GROUP, LANES), jnp.float32)]
        + same(values)
        + [sems(2, n), sems(12)],
        {1: 0},
        MOST,
    )


def added(there, last, base, first, row):
    return call(
        functools.partial(add_kernel, first, row),
        None,
        [there, last, base],
        [floats(*base.shape)],
        same([there]) + [sems(1)],
        {2: 0},
        MOST,
        2,
    )[0]


def added_half(there, last, base, first, mats):
    return call(
        functools.partial(half_kernel, first),
        None,
        [there, last, mats["rows_back"], mats["kept_back"], base],
        [floats(*base.shape)],
        [pltpu.VMEM((SPAN, GROUP, LANES), jnp.float32), sems(1)],
        {4: 0},
        MOST,
        4,
    )[0]


def decoded(payload, base, first, mats):
    values = [mats["rows_back"], mats["kept_back"]]
    count = payload.shape[0]
    return call(
        functools.partial(decode_kernel, first, count),
        None,
        [payload, *values, base],
        [floats(*base.shape)],
        [pltpu.VMEM((count, PAYLOAD, LANES), jnp.float32)]
        + held(count, jnp.float32)
        + lows(count)
        + same(values)
        + [sems(3, count), sems(2)],
        {3: 0},
        MOST,
    )[0]


def updated(place, band, scale, shape, mats):
    values = [mats["low_back"], mats["band_back"]]
    count = shape[1] // QUANTUM
    return call(
        functools.partial(update_kernel, scale, count),
        place,
        [band, *values],
        [floats(*shape)],
        same([band, *values]) + held(count, jnp.float32) + lows(count) + [sems(count), sems(3)],
        {},
        MOST,
    )[0]


def tiles(x):
    rows, mats, width = x.shape
    x = x.reshape(rows, mats, width // LANES, LANES).transpose(0, 2, 1, 3)
    return x.reshape(rows, mats * width // LANES, LANES)


def untiles(x, mats):
    rows, places, _ = x.shape
    x = x.reshape(rows, places // mats, mats, LANES).transpose(0, 2, 1, 3)
    return x.reshape(rows, mats, places // mats * LANES)


def tie(*arrays):
    return lax.optimization_barrier(arrays)


def per_device(grads, momentum):
    rep_count = lax.axis_size("rep")
    mat_count = grads.shape[3]
    mats = constants()
    g = tiles(grads[0, 0])
    m = tiles(momentum[0])
    count = m.shape[1] // QUANTUM
    member = lax.axis_index("fsdp")
    place = jnp.full((8, LANES), member, jnp.int32)
    over_core = [(f, f ^ 1) for f in range(4)]
    over_z = [(f, f ^ 2) for f in range(4)]

    def core(x):
        return lax.ppermute(x, "fsdp", over_core)

    def link(x):
        return lax.ppermute(x, "fsdp", over_z)

    def head(slot):
        return lax.dynamic_slice(g, ((member ^ slot) * SPAN, 0, 0), (SPAN, QUANTUM, LANES)).astype(jnp.float32)

    place1, cells = tie(place, head(3))
    more, own = cast(place1, g, (3, 1, SECOND), (2, 0, 1))
    got, more = tie(core(cells), more)
    cells = own + got
    early = link(cells)
    pay, other_band = encoded(place, g, [core(more)], 1, (SECOND,), 2, mats)
    second = link(pay)
    place2, _ = tie(place1, pay)
    wanted = [(3, k, 1) for k in range(1 + SECOND, count)] + [(1, k, 2) for k in range(0, count, 2)]
    *cells, later = cast(place2, g, *wanted)
    early, later, _ = tie(early, later, pay)
    pieces = [core(c) for c in [*cells, later]]
    got, mine = pieces[: -count // 2], pieces[-count // 2 :]
    pay, other_band = encoded(place, g, got, 1 + SECOND, (count - 2 - SECOND,), 2, mats, other_band)
    third = link(pay)
    names = ("rep", "fsdp")
    wrapped = lax.ppermute(other_band, names, steps(rep_count, 0, 2))
    cells, own_band = moments(place, m, g, early, mine, 0, mats)
    base, last, half, top, bottom = rest(place, cells, own_band, g, got[-1], 2, mats)

    groups = [[h * PLANE + i for i in range(PLANE)] for h in range(rep_count // PLANE)]
    met = lax.all_to_all(own_band + wrapped, "rep", 0, 0, axis_index_groups=groups, tiled=True)
    met, bottom = tie(met, bottom)
    half, top, bottom = link(half), link(top), link(bottom)
    part = jnp.sum(met.reshape(PLANE, QUARTER, LANES), axis=0)
    relayed = lax.ppermute(part, names, steps(rep_count, 0, 2))
    total = part + lax.ppermute(relayed, names, steps(rep_count, TURN, 2, plane=0))
    total, second = tie(total, second)
    spread = jnp.broadcast_to(total[None], (PLANE,) + total.shape)
    band_total = lax.all_to_all(spread, "rep", 0, 0, axis_index_groups=groups, tiled=True)
    out, band_total = tie(decoded(second, base, 1, mats), band_total)
    update = updated(place, band_total, 1.0 / rep_count, m.shape, mats)

    third, update = tie(third, update)
    out = decoded(third, out, 1 + SECOND, mats)
    half, out = tie(half, out)
    out = added_half(half, last, out, count - 1, mats)
    top, out = tie(top, out)
    out = added(top, last, out, count - 1, 0)
    bottom, out = tie(bottom, out)
    out = added(bottom, last, out, count - 1, SPLIT)
    return (untiles(out, mat_count)[None], untiles(update, mat_count))


def steps(rep_count, turn, member, plane=1):
    pairs = []
    for rep in range(rep_count):
        high, low = divmod(rep, PLANE)
        on = high == plane
        to = (high ^ plane) * PLANE + (low + (turn if on else PLANE - turn)) % PLANE
        pairs += [(rep * 4 + f, to * 4 + (f ^ member)) for f in range(4)]
    return pairs


def solution(mesh):
    in_specs = (P("rep", "fsdp", None, None, None), P("rep", "fsdp", None, None))
    out_specs = (P("rep", "fsdp", None, None), P("fsdp", None, None))
    return jax.shard_map(
        per_device, mesh=mesh, in_specs=in_specs, out_specs=out_specs, check_vma=False
    )
```

```python
import functools
import math

import jax
import jax.numpy as jnp
import ml_dtypes
import numpy as np
from jax import lax
from jax.experimental import pallas as pl
from jax.experimental.pallas import tpu as pltpu
from jax.sharding import PartitionSpec as P

SPAN = 64
BAND = 16
LANES = 128
GROUP = 8
QUANTUM = 2 * GROUP
DECAY = 0.9
HIGH = SPAN - BAND
QUARTER = GROUP // 4 * BAND
PAYLOAD = QUANTUM * HIGH + 3 * SPAN
SECOND = 4
SPLIT = 48
PLANE = 16
TURN = 4
MOST = 46


def dct(order):
    q = np.arange(order)[:, None]
    n = np.arange(order)[None, :]
    scale = np.where(q == 0, math.sqrt(1.0 / order), math.sqrt(2.0 / order))
    return scale * np.cos(math.pi * (2 * n + 1) * q / (2 * order))


def halves(a):
    high = a.astype(ml_dtypes.bfloat16)
    return high, (a - high.astype(np.float64)).astype(ml_dtypes.bfloat16)


def left(a):
    high, low = halves(a)
    return np.concatenate([high, low, high], axis=1)


def right(a):
    high, low = halves(a)
    return np.concatenate([high, low, high], axis=0)


def constants():
    t = dct(SPAN)
    lanes = np.kron(np.eye(8), t.T)
    coef = np.arange(512) % SPAN
    order = np.concatenate([np.flatnonzero(coef >= BAND), np.flatnonzero(coef < BAND)])
    lanes = lanes[:, order]
    kept, band = lanes[:, : 3 * LANES], lanes[:, 3 * LANES :]
    mats = dict(
        rows=left(t), rows_back=left(t.T), low=left(t[:BAND]), low_back=left(t[:BAND].T),
        lanes=right(lanes), kept=right(kept), kept_back=right(kept.T), band=right(band), band_back=right(band.T),
    )
    return {name: jnp.asarray(a) for name, a in mats.items()}


def split(x):
    high = x.astype(jnp.bfloat16)
    return high, (x - high.astype(jnp.float32)).astype(jnp.bfloat16)


def tall(x):
    high, low = split(x)
    return jnp.concatenate([high, high, low], axis=0)


def long(x):
    high, low = split(x)
    return jnp.concatenate([high, high, low], axis=1)


def dot(a, b):
    return jnp.dot(a, b, preferred_element_type=jnp.float32)


def beside(x):
    x = jnp.swapaxes(x, 0, 1)
    return [jnp.concatenate([x[4 * s + j] for j in range(4)], axis=1) for s in range(4)]


def apart(parts):
    x = jnp.stack([p[:, j * LANES : (j + 1) * LANES] for p in parts for j in range(4)], axis=0)
    return jnp.swapaxes(x, 0, 1)


def forward(x, rows):
    return [dot(rows, tall(part)) for part in beside(x)]


def back(parts, rows):
    return apart([dot(rows, tall(p)) for p in parts])


def bands_of(c):
    return [c[s * BAND : (s + 1) * BAND] for s in range(4)]


def rows_of(slot):
    member = lax.axis_index("fsdp") ^ slot
    return pl.ds(pl.multiple_of(member * SPAN, SPAN), SPAN)


def turn(other=False):
    own = lax.div(lax.axis_index("rep"), PLANE) * TURN
    return TURN - own if other else own


def quantum(k):
    return pl.ds(k * QUANTUM, QUANTUM)


def band_at(k, shift):
    return pl.ds(lax.rem(2 * k + PLANE - shift, PLANE), 2)


def load(constants, buffers, sems):
    copies = [pltpu.make_async_copy(c, b, sems.at[i]) for i, (c, b) in enumerate(zip(constants, buffers))]
    for copy in copies:
        copy.start()
    return copies


def cast_kernel(wanted, place, g_ref, *refs):
    outs, (held, sems) = refs[: len(wanted)], refs[len(wanted) :]
    where = [(o, j, slot, first + j) for o, (slot, first, n) in zip(outs, wanted) for j in range(n)]
    into = []
    for k, (_, _, slot, at) in enumerate(where):
        into.append(pltpu.make_async_copy(g_ref.at[rows_of(slot), quantum(at), :], held.at[k], sems.at[k]))
        into[-1].start()
    for k, (o, j, _, _) in enumerate(where):
        into[k].wait()
        o[:, j * QUANTUM : (j + 1) * QUANTUM, :] = held[k].astype(jnp.float32)


def encode_kernel(first, counts, extra, slot, received, place, g_ref, *refs):
    come = [(ref, j) for ref, n in zip(refs, received) for j in range(n)]
    rows, lanes, *refs = refs[len(received) :]
    refs = refs[extra:]
    pays, refs = refs[: len(counts)], refs[len(counts) :]
    band_ref, g_buf, r_buf, pay_buf, band_buf, low_buf, zero_buf, rows_buf, lanes_buf, sems, more_sems = refs
    high = QUANTUM * HIGH
    sent = sum(counts)
    count = sent + extra
    where = [(ref, j) for ref, n in zip(pays, counts) for j in range(n)]
    other_turn = turn(other=True)

    def into(k, ref=None, j=0):
        ref = come[0][0] if ref is None else ref
        yield pltpu.make_async_copy(g_ref.at[rows_of(slot), quantum(first + k), :], g_buf.at[k], sems.at[0, k])
        yield pltpu.make_async_copy(ref.at[:, quantum(j), :], r_buf.at[k], sems.at[1, k])

    def out_high(k, ref, j):
        at = pl.ds(0, high)
        return pltpu.make_async_copy(pay_buf.at[k, at], ref.at[j, at], sems.at[2, k])

    def out_low(k, ref, j):
        at = pl.ds(high, 3 * SPAN)
        return pltpu.make_async_copy(pay_buf.at[k, at], ref.at[j, at], sems.at[3, k])

    def out_band(k):
        return pltpu.make_async_copy(band_buf.at[k], band_ref.at[band_at(first + k, other_turn)], sems.at[4, k])

    if not extra:
        blank = pltpu.make_async_copy(zero_buf, band_ref.at[band_at(0, other_turn)], more_sems.at[2])
    for copy in into(0, *come[0]):
        copy.start()
    consts = load((rows, lanes), (rows_buf, lanes_buf), more_sems)
    for k in range(1, count):
        for copy in into(k, *come[k]):
            copy.start()
    if not extra:
        zero_buf[...] = jnp.zeros_like(zero_buf)
        blank.start()
    consts[0].wait()

    def low_of(k, c, s):
        low_buf[k, s * BAND : (s + 1) * BAND, :] = c[:BAND]

    def cells_of(k):
        for copy in into(k):
            copy.wait()
        return g_buf[k].astype(jnp.float32) + r_buf[k]

    def body(k, _):
        for s, c in enumerate(forward(cells_of(k), rows_buf[...])):
            low_of(k, c, s)
            for j in range(4):
                at = (4 * s + j) * HIGH
                pay_buf[k, at : at + HIGH, :] = c[BAND:, j * LANES : (j + 1) * LANES]
        for i, ref in enumerate(pays):
            start = sum(counts[:i])

            @pl.when((k >= start) & (k < start + counts[i]))
            def _():
                out_high(k, ref, k - start).start()

        return 0

    lax.fori_loop(0, sent, body, 0)
    for k in range(sent, count):
        for s, c in enumerate(forward(cells_of(k), rows_buf[:BAND, :])):
            low_of(k, c, s)
    consts[1].wait()
    w = dot(long(low_buf[...].reshape(count * SPAN, 4 * LANES)), lanes_buf[...])
    for k in range(count):
        part = w[k * SPAN : (k + 1) * SPAN]
        if k < sent:
            for i in range(3):
                at = high + i * SPAN
                pay_buf[k, at : at + SPAN, :] = part[:, i * LANES : (i + 1) * LANES]
            out_low(k, *where[k]).start()
        band_buf[k] = part[:, 3 * LANES :].reshape(2, QUARTER, LANES)
        out_band(k).start()
    for k in range(count):
        if k < sent:
            out_high(k, *where[k]).wait()
            out_low(k, *where[k]).wait()
        out_band(k).wait()
    if not extra:
        blank.wait()


def moment_kernel(counts, slot, place, m_ref, g_ref, early_ref, *refs):
    received, refs = refs[: len(counts)], refs[len(counts) :]
    constants, refs = refs[:2], refs[2:]
    cells_ref, band_ref, m_buf, g_buf, r_buf, band_buf, low_buf, early_buf = refs[:8]
    buffers, (sems, more_sems) = refs[8:10], refs[10:]
    own_turn = turn()
    total = sum(counts)
    where = [(r, j) for r, n in zip(received, counts) for j in range(n)]

    def into(k, r=None, j=0):
        r = received[0] if r is None else r
        yield pltpu.make_async_copy(g_ref.at[rows_of(slot), quantum(k), :], g_buf.at[k], sems.at[0, k])
        yield pltpu.make_async_copy(r.at[:, quantum(j), :], r_buf.at[k], sems.at[1, k])
        yield pltpu.make_async_copy(m_ref.at[:, quantum(k), :], m_buf.at[k], sems.at[2, k])

    def out(k):
        return pltpu.make_async_copy(m_buf.at[k], cells_ref.at[:, quantum(k), :], sems.at[3, k])

    def out_band(k):
        return pltpu.make_async_copy(band_buf.at[k], band_ref.at[band_at(k, own_turn)], sems.at[4, k])

    early = pltpu.make_async_copy(early_ref, early_buf, more_sems.at[2])
    for copy in (*into(0, *where[0]), early):
        copy.start()
    consts = load(constants, buffers, more_sems)
    for k in range(1, total):
        for copy in into(k, *where[k]):
            copy.start()
    for copy in consts:
        copy.wait()
    low, band = buffers

    def cells_of(k, more=None):
        for copy in into(k):
            copy.wait()
        cells = DECAY * m_buf[k] + (g_buf[k].astype(jnp.float32) + r_buf[k])
        if more is not None:
            cells = cells + more
        m_buf[k] = cells
        out(k).start()
        for s, c in enumerate(forward(cells, low[...])):
            low_buf[k, s * BAND : (s + 1) * BAND, :] = c

    def body(k, _):
        cells_of(k)
        return 0

    early.wait()
    cells_of(0, early_buf[...])
    lax.fori_loop(1, total, body, 0)
    b = dot(long(low_buf[...].reshape(total * SPAN, 4 * LANES)), band[...])
    band_buf[...] = b.reshape(total, 2, QUARTER, LANES)
    for k in range(total):
        out_band(k).start()
    for k in range(total):
        out(k).wait()
        out_band(k).wait()


def rest_kernel(slot, place, cells_ref, bands_ref, g_ref, r_ref, *refs):
    constants, refs = refs[:5], refs[5:]
    out_ref, last_ref, half_ref, top_ref, bottom_ref = refs[:5]
    cells_buf, band_buf, low_buf, g_buf, r_buf, half_buf, raw_buf = refs[5:12]
    buffers, (sems, more_sems) = refs[12:17], refs[17:]
    own_turn = turn()
    total = cells_buf.shape[0]
    split = top_ref.shape[0]

    def into(k):
        return pltpu.make_async_copy(cells_ref.at[:, quantum(k), :], cells_buf.at[k], sems.at[0, k])

    def out(k):
        return pltpu.make_async_copy(cells_buf.at[k], out_ref.at[:, quantum(k), :], sems.at[1, k])

    def out_last():
        yield pltpu.make_async_copy(cells_buf.at[total - 1], last_ref, more_sems.at[5])
        yield pltpu.make_async_copy(half_buf, half_ref, more_sems.at[6])
        yield pltpu.make_async_copy(raw_buf.at[pl.ds(0, split)], top_ref, more_sems.at[7])
        yield pltpu.make_async_copy(raw_buf.at[pl.ds(split, SPAN - split)], bottom_ref, more_sems.at[8])

    copies = [
        pltpu.make_async_copy(g_ref.at[rows_of(slot), quantum(total - 1), :], g_buf, more_sems.at[9]),
        pltpu.make_async_copy(r_ref.at[:, quantum(r_ref.shape[1] // QUANTUM - 1), :], r_buf, more_sems.at[10]),
        pltpu.make_async_copy(bands_ref, band_buf, more_sems.at[11]),
    ]
    for copy in copies:
        copy.start()
    consts = load(constants, buffers, more_sems)
    for k in range(total):
        into(k).start()
    for copy in (*copies, *consts):
        copy.wait()
    rows, kept, low_back, band, band_back = buffers

    theirs = g_buf[...].astype(jnp.float32) + r_buf[...]
    c = []
    for s, x in enumerate(beside(theirs)):
        c.append(dot(rows[...] if s < 2 else rows[:BAND, :], tall(x)))
    for k in range(GROUP):
        half_buf[k * HIGH : (k + 1) * HIGH, :] = c[k // 4][BAND:, k % 4 * LANES : (k % 4 + 1) * LANES]
    w = dot(long(jnp.concatenate([c[0][:BAND], c[1][:BAND]], axis=0)), kept[...])
    for i in range(3):
        at = GROUP * HIGH + i * QUARTER
        half_buf[at : at + QUARTER, :] = w[:, i * LANES : (i + 1) * LANES]
    theirs_band = dot(long(jnp.concatenate(c[2:], axis=0)), band[...])
    b = jnp.concatenate([band_buf[...].reshape(total * SPAN, LANES), theirs_band], axis=0)
    wide = dot(long(b), band_back[...])
    low_buf[...] = wide[: total * SPAN].reshape(total, SPAN, 4 * LANES)
    low = wide[total * SPAN :]
    raw_buf[...] = theirs[:, GROUP:, :] - back([low[:BAND], low[BAND:]], low_back[...])

    def body(k, _):
        into(k).wait()
        turned = lax.rem(k + total - lax.div(own_turn, 2), total)
        cells_buf[k] = cells_buf[k] - back(bands_of(low_buf[turned]), low_back[...])

        @pl.when(k < total - 1)
        def _():
            out(k).start()

        return 0

    lax.fori_loop(0, total, body, 0)
    for copy in out_last():
        copy.start()
    for k in range(total - 1):
        out(k).wait()
    for copy in out_last():
        copy.wait()


def decode_kernel(first, count, pay_ref, rows_back, kept_back, base_ref, out_ref, *refs):
    pay_buf, base_buf, low_buf, rows_buf, kept_buf, sems, const_sems = refs
    at = QUANTUM * HIGH

    def into(k):
        yield pltpu.make_async_copy(pay_ref.at[k], pay_buf.at[k], sems.at[0, k])
        yield pltpu.make_async_copy(base_ref.at[:, quantum(first + k), :], base_buf.at[k], sems.at[1, k])

    def out(k):
        return pltpu.make_async_copy(base_buf.at[k], out_ref.at[:, quantum(first + k), :], sems.at[2, k])

    for k in range(count):
        for copy in into(k):
            copy.start()
    for copy in load((rows_back, kept_back), (rows_buf, kept_buf), const_sems):
        copy.wait()
    for k in range(count):
        for copy in into(k):
            copy.wait()
    kept = [
        jnp.concatenate([pay_buf[k, at + i * SPAN : at + (i + 1) * SPAN, :] for i in range(3)], axis=1)
        for k in range(count)
    ]
    low_buf[...] = dot(long(jnp.concatenate(kept, axis=0)), kept_buf[...]).reshape(count, SPAN, 4 * LANES)

    def body(k, _):
        parts = []
        for s, low in enumerate(bands_of(low_buf[k])):
            high = [pay_buf[k, (4 * s + j) * HIGH : (4 * s + j + 1) * HIGH, :] for j in range(4)]
            parts.append(jnp.concatenate([low, jnp.concatenate(high, axis=1)], axis=0))
        base_buf[k] = base_buf[k] + back(parts, rows_buf[...])
        out(k).start()
        return 0

    lax.fori_loop(0, count, body, 0)
    for k in range(count):
        out(k).wait()


def add_kernel(first, row, there_ref, last_ref, base_ref, out_ref, sum_buf, sem):
    rows = pl.ds(row, there_ref.shape[0])
    sum_buf[...] = last_ref[rows, GROUP:, :] + there_ref[...]
    out = pltpu.make_async_copy(sum_buf, out_ref.at[rows, pl.ds(first * QUANTUM + GROUP, GROUP)], sem.at[0])
    out.start()
    out.wait()


def half_kernel(first, half_ref, last_ref, rows_back, kept_back, base_ref, out_ref, sum_buf, sem):
    at = GROUP * HIGH
    w = jnp.concatenate([half_ref[at + i * QUARTER : at + (i + 1) * QUARTER, :] for i in range(3)], axis=1)
    low = dot(long(w), kept_back[...])
    parts = []
    for s in range(2):
        high = [half_ref[k * HIGH : (k + 1) * HIGH, :] for k in range(4 * s, 4 * s + 4)]
        parts.append(jnp.concatenate([low[s * BAND : (s + 1) * BAND], jnp.concatenate(high, axis=1)], axis=0))
    sum_buf[...] = last_ref[:, :GROUP, :] + back(parts, rows_back[...])
    out = pltpu.make_async_copy(sum_buf, out_ref.at[:, pl.ds(first * QUANTUM, GROUP)], sem.at[0])
    out.start()
    out.wait()


def update_kernel(scale, count, place, band_ref, low_back, band_back, out_ref, band_buf, low_rows, back_buf, out_buf, low_buf, sems, const_sems):
    own_turn = turn()
    for copy in load((band_ref, low_back, band_back), (band_buf, low_rows, back_buf), const_sems):
        copy.wait()
    b = band_buf[...].reshape(count * SPAN, LANES) * scale
    low_buf[...] = dot(long(b), back_buf[...]).reshape(count, SPAN, 4 * LANES)

    def out(k):
        return pltpu.make_async_copy(out_buf.at[k], out_ref.at[:, quantum(k), :], sems.at[k])

    def body(k, _):
        turned = lax.rem(k + count - lax.div(own_turn, 2), count)
        out_buf[k] = back(bands_of(low_buf[turned]), low_rows[...])
        out(k).start()
        return 0

    lax.fori_loop(0, count, body, 0)
    for k in range(count):
        out(k).wait()


ANY = pl.BlockSpec(memory_space=pl.ANY)
BANDS = jax.ShapeDtypeStruct((PLANE, QUARTER, LANES), jnp.float32)


def call(kernel, place, operands, outs, scratch, aliases, vmem, near=0, out_spec=ANY):
    operands = operands if place is None else [place, *operands]
    return pl.pallas_call(
        kernel,
        grid_spec=pltpu.PrefetchScalarGridSpec(
            num_scalar_prefetch=0,
            grid=(),
            in_specs=[pl.BlockSpec(memory_space=pltpu.VMEM)] * near + [ANY] * (len(operands) - near),
            out_specs=[out_spec] * len(outs),
            scratch_shapes=scratch,
        ),
        out_shape=outs,
        input_output_aliases=aliases,
        cost_estimate=pl.CostEstimate(flops=0, bytes_accessed=0, transcendentals=0),
        compiler_params=pltpu.CompilerParams(vmem_limit_bytes=vmem * 1024 * 1024),
    )(*operands)


def floats(*shape):
    return jax.ShapeDtypeStruct(shape, jnp.float32)


def held(count, *dtypes):
    return [pltpu.VMEM((count, SPAN, QUANTUM, LANES), dtype) for dtype in dtypes]


def lows(count):
    return [pltpu.VMEM((count, SPAN, 4 * LANES), jnp.float32)]


def same(arrays):
    return [pltpu.VMEM(a.shape, a.dtype) for a in arrays]


def sems(*shape):
    return pltpu.SemaphoreType.DMA(shape)


def cast(place, g, *wanted):
    n = sum(count for _, _, count in wanted)
    return call(
        functools.partial(cast_kernel, wanted),
        place,
        [g],
        [floats(SPAN, count * QUANTUM, LANES) for _, _, count in wanted],
        held(n, jnp.bfloat16) + [sems(n)],
        {},
        MOST,
        out_spec=pl.BlockSpec(memory_space=pltpu.VMEM),
    )


def encoded(place, g, received, first, counts, slot, mats, bands=None):
    values = [mats["rows"], mats["lanes"]]
    extra = int(bands is not None)
    sent = sum(counts)
    n = sent + extra
    return call(
        functools.partial(encode_kernel, first, counts, extra, slot, [r.shape[1] // QUANTUM for r in received]),
        place,
        [g, *received, *values, *([bands] * extra)],
        [floats(c, PAYLOAD, LANES) for c in counts] + [BANDS],
        held(n, jnp.bfloat16, jnp.float32)
        + [pltpu.VMEM((sent, PAYLOAD, LANES), jnp.float32), pltpu.VMEM((n, 2, QUARTER, LANES), jnp.float32)]
        + lows(n)
        + [pltpu.VMEM((2, QUARTER, LANES), jnp.float32)]
        + same(values)
        + [sems(5, n), sems(3)],
        {4 + len(received): len(counts)} if extra else {},
        MOST,
    )


def moments(place, m, g, early, received, slot, mats):
    values = [mats["low"], mats["band"]]
    counts = [r.shape[1] // QUANTUM for r in received]
    n = sum(counts)
    return call(
        functools.partial(moment_kernel, counts, slot),
        place,
        [m, g, early, *received, *values],
        [floats(*m.shape), BANDS],
        held(n, jnp.float32, jnp.bfloat16, jnp.float32)
        + [pltpu.VMEM((n, 2, QUARTER, LANES), jnp.float32)]
        + lows(n)
        + [pltpu.VMEM((SPAN, QUANTUM, LANES), jnp.float32)]
        + same(values)
        + [sems(5, n), sems(3)],
        {},
        MOST,
    )


def rest(place, cells, bands, g, received, slot, mats):
    values = [mats[name] for name in ("rows", "kept", "low_back", "band", "band_back")]
    n = cells.shape[1] // QUANTUM
    half = (GROUP * HIGH + 3 * QUARTER, LANES)
    return call(
        functools.partial(rest_kernel, slot),
        place,
        [cells, bands, g, received, *values],
        [
            floats(*cells.shape),
            floats(SPAN, QUANTUM, LANES),
            floats(*half),
            floats(SPLIT, GROUP, LANES),
            floats(SPAN - SPLIT, GROUP, LANES),
        ],
        held(n, jnp.float32)
        + [pltpu.VMEM(BANDS.shape, jnp.float32)]
        + lows(n)
        + [pltpu.VMEM((SPAN, QUANTUM, LANES), dtype) for dtype in (jnp.bfloat16, jnp.float32)]
        + [pltpu.VMEM(half, jnp.float32), pltpu.VMEM((SPAN, GROUP, LANES), jnp.float32)]
        + same(values)
        + [sems(2, n), sems(12)],
        {1: 0},
        MOST,
    )


def added(there, last, base, first, row):
    return call(
        functools.partial(add_kernel, first, row),
        None,
        [there, last, base],
        [floats(*base.shape)],
        same([there]) + [sems(1)],
        {2: 0},
        MOST,
        2,
    )[0]


def added_half(there, last, base, first, mats):
    return call(
        functools.partial(half_kernel, first),
        None,
        [there, last, mats["rows_back"], mats["kept_back"], base],
        [floats(*base.shape)],
        [pltpu.VMEM((SPAN, GROUP, LANES), jnp.float32), sems(1)],
        {4: 0},
        MOST,
        4,
    )[0]


def decoded(payload, base, first, mats):
    values = [mats["rows_back"], mats["kept_back"]]
    count = payload.shape[0]
    return call(
        functools.partial(decode_kernel, first, count),
        None,
        [payload, *values, base],
        [floats(*base.shape)],
        [pltpu.VMEM((count, PAYLOAD, LANES), jnp.float32)]
        + held(count, jnp.float32)
        + lows(count)
        + same(values)
        + [sems(3, count), sems(2)],
        {3: 0},
        MOST,
    )[0]


def updated(place, band, scale, shape, mats):
    values = [mats["low_back"], mats["band_back"]]
    count = shape[1] // QUANTUM
    return call(
        functools.partial(update_kernel, scale, count),
        place,
        [band, *values],
        [floats(*shape)],
        same([band, *values]) + held(count, jnp.float32) + lows(count) + [sems(count), sems(3)],
        {},
        MOST,
    )[0]


def tiles(x):
    rows, mats, width = x.shape
    x = x.reshape(rows, mats, width // LANES, LANES).transpose(0, 2, 1, 3)
    return x.reshape(rows, mats * width // LANES, LANES)


def untiles(x, mats):
    rows, places, _ = x.shape
    x = x.reshape(rows, places // mats, mats, LANES).transpose(0, 2, 1, 3)
    return x.reshape(rows, mats, places // mats * LANES)


def tie(*arrays):
    return lax.optimization_barrier(arrays)


def per_device(grads, momentum):
    rep_count = lax.axis_size("rep")
    mat_count = grads.shape[3]
    mats = constants()
    g = tiles(grads[0, 0])
    m = tiles(momentum[0])
    count = m.shape[1] // QUANTUM
    member = lax.axis_index("fsdp")
    place = jnp.full((8, LANES), member, jnp.int32)
    over_core = [(f, f ^ 1) for f in range(4)]
    over_z = [(f, f ^ 2) for f in range(4)]

    def core(x):
        return lax.ppermute(x, "fsdp", over_core)

    def link(x):
        return lax.ppermute(x, "fsdp", over_z)

    def head(slot):
        return lax.dynamic_slice(g, ((member ^ slot) * SPAN, 0, 0), (SPAN, QUANTUM, LANES)).astype(jnp.float32)

    place1, cells = tie(place, head(3))
    more, own = cast(place1, g, (3, 1, SECOND), (2, 0, 1))
    got, more = tie(core(cells), more)
    cells = own + got
    early = link(cells)
    pay, other_band = encoded(place, g, [core(more)], 1, (SECOND,), 2, mats)
    second = link(pay)
    place2, _ = tie(place1, pay)
    wanted = [(3, k, 1) for k in range(1 + SECOND, count)] + [(1, k, 2) for k in range(0, count, 2)]
    *cells, later = cast(place2, g, *wanted)
    early, later, _ = tie(early, later, pay)
    pieces = [core(c) for c in [*cells, later]]
    got, mine = pieces[: -count // 2], pieces[-count // 2 :]
    pay, other_band = encoded(place, g, got, 1 + SECOND, (count - 2 - SECOND,), 2, mats, other_band)
    third = link(pay)
    names = ("rep", "fsdp")
    wrapped = lax.ppermute(other_band, names, steps(rep_count, 0, 2))
    cells, own_band = moments(place, m, g, early, mine, 0, mats)
    base, last, half, top, bottom = rest(place, cells, own_band, g, got[-1], 2, mats)

    groups = [[h * PLANE + i for i in range(PLANE)] for h in range(rep_count // PLANE)]
    met = lax.all_to_all(own_band + wrapped, "rep", 0, 0, axis_index_groups=groups, tiled=True)
    met, bottom = tie(met, bottom)
    half, top, bottom = link(half), link(top), link(bottom)
    part = jnp.sum(met.reshape(PLANE, QUARTER, LANES), axis=0)
    total = part + lax.ppermute(part, names, steps(rep_count, TURN, 0))
    total, second = tie(total, second)
    spread = jnp.broadcast_to(total[None], (PLANE,) + total.shape)
    band_total = lax.all_to_all(spread, "rep", 0, 0, axis_index_groups=groups, tiled=True)
    out, band_total = tie(decoded(second, base, 1, mats), band_total)
    update = updated(place, band_total, 1.0 / rep_count, m.shape, mats)

    third, update = tie(third, update)
    out = decoded(third, out, 1 + SECOND, mats)
    half, out = tie(half, out)
    out = added_half(half, last, out, count - 1, mats)
    top, out = tie(top, out)
    out = added(top, last, out, count - 1, 0)
    bottom, out = tie(bottom, out)
    out = added(bottom, last, out, count - 1, SPLIT)
    return (untiles(out, mat_count)[None], untiles(update, mat_count))


def steps(rep_count, turn, member):
    pairs = []
    for rep in range(rep_count):
        high, low = divmod(rep, PLANE)
        to = (high ^ 1) * PLANE + (low + (turn if high else PLANE - turn)) % PLANE
        pairs += [(rep * 4 + f, to * 4 + (f ^ member)) for f in range(4)]
    return pairs


def solution(mesh):
    in_specs = (P("rep", "fsdp", None, None, None), P("rep", "fsdp", None, None))
    out_specs = (P("rep", "fsdp", None, None), P("fsdp", None, None))
    return jax.shard_map(
        per_device, mesh=mesh, in_specs=in_specs, out_specs=out_specs, check_vma=False
    )
```
